256 devices in a mesh: ctx: 32 (over y, z), head: 8 (over x, core).
Axes of the slice: x: 4, y: 4, z: 8, core: 2. Of those that a mesh axis runs over, the one named last changes fastest.
Arguments:
- queries: bfloat16 [16384, 40, 128], P(('ctx', 'head')), may hold values from -40 to 40
- keys: bfloat16 [16384, 8, 128], P(('ctx', 'head')), may hold values from -6 to 6
- values: bfloat16 [16384, 8, 128], P(('ctx', 'head')), may hold values from -6 to 6
- out_grad: bfloat16 [16384, 40, 128], P(('ctx', 'head')), may hold values from -6 to 6
- ancestors: int32 [128, 16], replicated, may hold values from -1 to 126, as said below
- parents: int32 [128, 128], P('ctx'), may hold values from 0 to 126, as said below
Outputs:
- attended: bfloat16 [16384, 40, 128], P(('ctx', 'head'))
- query_grad: bfloat16 [16384, 40, 128], P(('ctx', 'head'))
- key_grad: bfloat16 [16384, 8, 128], P(('ctx', 'head'))
- value_grad: bfloat16 [16384, 8, 128], P(('ctx', 'head'))
The draws below stay inside these ranges and needn't reach their ends.
Inputs may be any that keep to these rules, and one draw needn't show every extreme that they name: Row b holds block b's ancestor blocks, the root first and one a depth, then -1. Block 0 is the root; every other row begins with 0. Every ancestor of block b is block b - 1 or an ancestor of block b - 1. The last block has exactly 16 ancestors. parents[b, 0] = 0 and parents[b, t] < t for t > 0; parents[b, 127] = 126.
All inputs are finite; a program needn't handle non-finite values.
Results may differ from the reference program's by a relative error of at most 0.017.
The reference program's roundings to bfloat16 on the way (of `weights` and `dscore`) count: a program that leaves them out, or rounds other values in their place, can miss the bound.
Values may be sent and summed in bfloat16 or wider, within the bound.
No kernel may reach another device: no remote copies, remote signals or barrier semaphores. Data moves between devices by JAX's collectives and lax.ppermute only.
A program may use at most 192 MiB of HBM per device.

```python
import math
import jax
import jax.numpy as jnp
from jax import lax

HQ = 40
KVH = 8
HD = 128
GROUP = 5
BLK = 128
MAXD = 16
NB = 128
TOKENS = 16384


def shared_normals(key):
    return jax.random.normal(key, (TOKENS, KVH, HD), jnp.float32)


def draw_keys(key, part):
    raw_keys = shared_normals(key)
    return jnp.clip(raw_keys, -6.0, 6.0).astype(jnp.bfloat16)


def draw_queries(key, part):
    key = jax.random.fold_in(key, 7)
    result = jnp.clip(jax.random.normal(key, (TOKENS, KVH, GROUP, HD), jnp.float32), -6.0, 6.0)
    return result.reshape(TOKENS, HQ, HD).astype(jnp.bfloat16)


def draw_parents(key, part):
    key = jax.random.fold_in(key, 21)
    first_key, second_key = jax.random.split(key)
    position = jnp.arange(BLK, dtype=jnp.int32)
    coin_flip = jax.random.randint(first_key, (NB, BLK), 0, 4)
    picked = jax.random.randint(second_key, (NB, BLK), 0, jnp.maximum(position, 1)[None, :])
    chained = jnp.maximum(position - 1, 0)[None, :]
    forced = (coin_flip > 0) | (position[None, :] == BLK - 1)
    return jnp.where(forced, chained, picked).astype(jnp.int32)


def draw_ancestors(key, part):
    key = jax.random.fold_in(key, 33)
    first_key, second_key = jax.random.split(key)
    coin_flip = jax.random.randint(first_key, (NB,), 0, 4)
    picked = jax.random.randint(second_key, (NB,), 0, MAXD + 1)
    depth_range = jnp.arange(MAXD, dtype=jnp.int32)

    def grow(carry, inputs):
        open_path, depth_prev = carry
        block_id, coin_now, pick_now = inputs
        keep_on = (coin_now > 0) | (block_id > NB - MAXD)
        parent_depth = jnp.where(keep_on, depth_prev, pick_now % (depth_prev + 1))
        parent_depth = jnp.where(block_id == NB - MAXD, 0, parent_depth)
        parent_depth = jnp.minimum(parent_depth, MAXD - 1)
        new_depth = parent_depth + 1
        open_path = open_path.at[new_depth].set(block_id)
        row_ids = jnp.where(depth_range < new_depth, open_path[:MAXD], -1)
        return ((open_path, new_depth), row_ids)
    start_path = jnp.zeros((MAXD + 1,), jnp.int32)
    block_ids = jnp.arange(1, NB, dtype=jnp.int32)
    final_state, rows = lax.scan(grow, (start_path, jnp.zeros((), jnp.int32)), (block_ids, coin_flip[1:], picked[1:]))
    return jnp.concatenate([jnp.full((1, MAXD), -1, jnp.int32), rows], axis=0)


def block_scale(own_key, extent, cuts, least, top_value):
    level = 1.0
    for dim, shards_of in cuts:
        heights = jax.random.uniform(jax.random.fold_in(jax.random.fold_in(own_key, 6), dim), (shards_of,), jnp.float32, least / len(cuts), top_value / len(cuts))
        level = level * jnp.repeat(jnp.exp(heights), extent[dim] // shards_of).reshape((-1,) + (1,) * (len(extent) - 1 - dim))
    return level


def normal_values(stream_key, extent, deviation, bound, cuts=(), kind=jnp.bfloat16):
    values = jax.random.normal(stream_key, extent, jnp.float32) * deviation
    if len(cuts) > 0:
        values = block_scale(stream_key, extent, cuts, -0.22, 0.18) * values
    return jnp.clip(values, min=-bound, max=bound).astype(kind)


def setup_inputs(seed: int = 0) -> dict:
    streams_of = jax.random.split(jax.random.key(seed), 7)
    queries = draw_queries(jax.random.fold_in(streams_of[6], 71), 0)
    keys = draw_keys(jax.random.fold_in(streams_of[6], 71), 0)
    values = normal_values(streams_of[2], (TOKENS, KVH, HD), 1.0, 6.0, ((0, 256),))
    out_grad = normal_values(streams_of[3], (TOKENS, HQ, HD), 1.0, 6.0, ((0, 256),))
    ancestors = draw_ancestors(jax.random.fold_in(streams_of[6], 71), 0)
    parents = draw_parents(jax.random.fold_in(streams_of[6], 71), 0)
    return {"queries": queries, "keys": keys, "values": values, "out_grad": out_grad, "ancestors": ancestors, "parents": parents}


def tree_reach(parents):
    block_width = parents.shape[-1]
    parent_hops = (parents[..., None] == jnp.arange(block_width, dtype=jnp.int32)).astype(jnp.float32)
    reached = jnp.minimum(jnp.eye(block_width, dtype=jnp.float32) + parent_hops, 1.0)
    for repeat_no in range(max(1, (block_width - 1).bit_length())):
        reached = jnp.minimum(jnp.einsum('bts,bsu->btu', reached, reached, precision=lax.Precision.HIGHEST), 1.0)
    return reached

def reference(queries, keys, values, out_grad, ancestors, parents):
    score_scale = 1.0 / math.sqrt(HD)
    query_blocks = queries.reshape(NB, BLK, KVH, GROUP, HD)
    grad_blocks = out_grad.reshape(NB, BLK, KVH, GROUP, HD)
    key_blocks = keys.reshape(NB, BLK, KVH, HD)
    value_blocks = values.reshape(NB, BLK, KVH, HD)
    within_all = tree_reach(parents) > 0.5
    slot_count = MAXD + 1

    def one_block(carry, block_id):
        key_acc, value_acc = carry
        listed = ancestors[block_id] >= 0
        chosen = jnp.concatenate([jnp.where(listed, ancestors[block_id], 0).astype(jnp.int32), block_id[None].astype(jnp.int32)])
        key_rows = key_blocks[chosen].astype(jnp.float32).reshape(slot_count * BLK, KVH, HD)
        value_rows = value_blocks[chosen].astype(jnp.float32).reshape(slot_count * BLK, KVH, HD)
        seen_far = jnp.broadcast_to(jnp.repeat(listed, BLK)[None, :], (BLK, MAXD * BLK))
        seen = jnp.concatenate([seen_far, within_all[block_id]], axis=1)
        query_rows = query_blocks[block_id].astype(jnp.float32)
        grad_rows = grad_blocks[block_id].astype(jnp.float32)
        scores = jnp.einsum('qgrd,kgd->grqk', query_rows, key_rows) * score_scale
        scores = jnp.where(seen[None, None], scores, -jnp.inf)
        row_max = lax.optimization_barrier(jnp.max(scores, axis=-1, keepdims=True))
        exponent = jnp.exp(scores - row_max)
        probs = exponent / lax.optimization_barrier(jnp.sum(exponent, axis=-1, keepdims=True))
        weights = lax.optimization_barrier(probs.astype(jnp.bfloat16)).astype(jnp.float32)
        attended = jnp.einsum('grqk,kgd->qgrd', weights, value_rows).astype(jnp.bfloat16)
        delta = jnp.einsum('qgrd,qgrd->grq', grad_rows, attended.astype(jnp.float32))
        dprob = jnp.einsum('qgrd,kgd->grqk', grad_rows, value_rows)
        dscore = lax.optimization_barrier((probs * (dprob - delta[..., None])).astype(jnp.bfloat16)).astype(jnp.float32)
        query_grad = (jnp.einsum('grqk,kgd->qgrd', dscore, key_rows) * score_scale).astype(jnp.bfloat16)
        key_part = (jnp.einsum('grqk,qgrd->kgd', dscore, query_rows) * score_scale).reshape(slot_count, BLK, KVH, HD)
        value_part = jnp.einsum('grqk,qgrd->kgd', weights, grad_rows).reshape(slot_count, BLK, KVH, HD)
        keep_rows = jnp.concatenate([listed, jnp.ones((1,), dtype=jnp.bool_)]).astype(jnp.float32)[:, None, None, None]
        key_acc = key_acc.at[chosen].add(key_part * keep_rows)
        value_acc = value_acc.at[chosen].add(value_part * keep_rows)
        return ((key_acc, value_acc), (attended, query_grad))
    zero_grads = jnp.zeros((NB, BLK, KVH, HD), jnp.float32)
    totals, outputs = lax.scan(one_block, (zero_grads, zero_grads), jnp.arange(NB, dtype=jnp.int32))
    attended = outputs[0].reshape(TOKENS, HQ, HD)
    query_grad = outputs[1].reshape(TOKENS, HQ, HD)
    key_grad = totals[0].astype(jnp.bfloat16).reshape(TOKENS, KVH, HD)
    value_grad = totals[1].astype(jnp.bfloat16).reshape(TOKENS, KVH, HD)
    return (attended, query_grad, key_grad, value_grad)
```

```python
import math

import jax
import jax.numpy as jnp
from jax import lax
from jax.experimental import pallas as pl
from jax.experimental.pallas import tpu as pltpu
from jax.sharding import Mesh, PartitionSpec as P

HD = 128
GROUP = 5
BLK = 128
NBL = 4
MAXD = 16
QN = GROUP * BLK
SCALE = 1.0 / math.sqrt(HD)
LOG2E = 1.0 / math.log(2.0)
NEG = -1e30
NPAIR = MAXD // 2 + NBL // 2
OWNP = MAXD // 2


def tree_reach_t(parents):
    block_width = parents.shape[-1]
    hops = parents[:, None, :] == jnp.arange(block_width, dtype=jnp.int32)[None, :, None]
    eye = jnp.eye(block_width, dtype=jnp.bool_)[None]
    reached = (hops | eye).astype(jnp.bfloat16)
    for _ in range(max(1, (block_width - 1).bit_length())):
        product = jnp.einsum("bts,bsu->btu", reached, reached, preferred_element_type=jnp.float32)
        reached = jnp.minimum(product, 1.0).astype(jnp.bfloat16)
    return reached.astype(jnp.float32)


def dot(a, b, dims):
    return lax.dot_general(a, b, (dims, ((), ())), preferred_element_type=jnp.float32)


def kernel(
    info_ref, q_ref, g_ref, own_ref, pool_ref, within_ref,
    o_ref, dq_ref, grad_ref,
    k_s, v_s, kt_s, vt_s, s_s, w_s, dk_s, dv_s,
):
    grad_ref[...] = jnp.zeros_like(grad_ref)
    dk_s[...] = jnp.zeros_like(dk_s)
    dv_s[...] = jnp.zeros_like(dv_s)
    remote = info_ref[0, 0]
    pairs = (remote + 1) // 2

    def take(p, half, kv):
        k = kv[:, 0].reshape(BLK, HD)
        v = kv[:, 1].reshape(BLK, HD)
        k_s[p, half * BLK:(half + 1) * BLK, :] = k
        v_s[p, half * BLK:(half + 1) * BLK, :] = v
        kt_s[p, :, half * BLK:(half + 1) * BLK] = k.T
        vt_s[p, :, half * BLK:(half + 1) * BLK] = v.T

    for j in range(NBL):
        take(OWNP + j // 2, j % 2, own_ref[j])

    def load_pair(p, carry):
        for half in range(2):
            block = info_ref[1, 2 * p + half]
            take(p, half, pool_ref[block])
        return carry

    lax.fori_loop(0, pairs, load_pair, 0)

    for i in range(NBL):
        rows = pl.ds(i * BLK, BLK)
        count = info_ref[2 + i, 0]
        my_pairs = (count + 1) // 2
        q = jnp.concatenate([q_ref[rows, r * HD:(r + 1) * HD] for r in range(GROUP)], axis=0)
        g = jnp.concatenate([g_ref[rows, r * HD:(r + 1) * HD] for r in range(GROUP)], axis=0)
        qt = q.T
        gt = g.T
        row_id = lax.broadcasted_iota(jnp.int32, (2 * BLK, 1), 0)

        def fold(x, op):
            y = x.reshape(-1, 8, QN)
            return op(y, axis=0)

        def scores(p, mx):
            raw = dot(k_s[p], qt, ((1,), (0,))) * (SCALE * LOG2E)
            limit = jnp.where(2 * p + 1 < count, 2 * BLK, BLK)
            s = raw + jnp.where(row_id < limit, 0.0, NEG)
            s_s[p] = s
            return jnp.maximum(mx, fold(s, jnp.max))

        mx = lax.fori_loop(0, my_pairs, scores, jnp.full((8, QN), NEG, jnp.float32))
        own_pairs = i // 2 + 1
        for op in range(own_pairs):
            raw = dot(k_s[OWNP + op], qt, ((1,), (0,))) * (SCALE * LOG2E)
            parts = []
            for half in range(2):
                j = 2 * op + half
                piece = raw[half * BLK:(half + 1) * BLK]
                if j < i:
                    piece = piece + jnp.where(info_ref[2 + i, 1 + j] > 0, 0.0, NEG)
                elif j == i:
                    bias = jnp.where(within_ref[i] > 0.5, 0.0, NEG)
                    piece = piece + jnp.concatenate([bias] * GROUP, axis=1)
                else:
                    piece = jnp.full_like(piece, NEG)
                parts.append(piece)
            s = jnp.concatenate(parts, axis=0)
            s_s[OWNP + op] = s
            mx = jnp.maximum(mx, fold(s, jnp.max))
        m = jnp.max(mx, axis=0, keepdims=True)

        def expo(p, total):
            e = jnp.exp2(s_s[p] - m)
            s_s[p] = e
            return total + fold(e, jnp.sum)

        total = lax.fori_loop(0, my_pairs, expo, jnp.zeros((8, QN), jnp.float32))
        for op in range(own_pairs):
            total = expo(OWNP + op, total)
        inv = 1.0 / jnp.sum(total, axis=0, keepdims=True)

        def attend(p, acc):
            prob = s_s[p] * inv
            s_s[p] = prob
            w = prob.astype(jnp.bfloat16)
            dv_s[p] += dot(w, g, ((1,), (0,)))
            return acc + dot(vt_s[p], w, ((1,), (0,)))

        acc = lax.fori_loop(0, my_pairs, attend, jnp.zeros((HD, QN), jnp.float32))
        for op in range(own_pairs):
            acc = attend(OWNP + op, acc)
        ot = acc.astype(jnp.bfloat16)
        delta = jnp.sum(gt.astype(jnp.float32) * ot.astype(jnp.float32), axis=0, keepdims=True)
        for r in range(GROUP):
            o_ref[rows, r * HD:(r + 1) * HD] = ot[:, r * BLK:(r + 1) * BLK].T

        def back(p, acc):
            dprob = dot(v_s[p], gt, ((1,), (0,)))
            ds = (s_s[p] * (dprob - delta)).astype(jnp.bfloat16)
            dk_s[p] += dot(ds, q, ((1,), (0,)))
            return acc + dot(kt_s[p], ds, ((1,), (0,)))

        acc = lax.fori_loop(0, my_pairs, back, jnp.zeros((HD, QN), jnp.float32))
        for op in range(own_pairs):
            acc = back(OWNP + op, acc)
        dqt = (acc * SCALE).astype(jnp.bfloat16)
        for r in range(GROUP):
            dq_ref[rows, r * HD:(r + 1) * HD] = dqt[:, r * BLK:(r + 1) * BLK].T

    def put(block, p, half):
        dk = dk_s[p, pl.ds(half * BLK, BLK), :] * SCALE
        dv = dv_s[p, pl.ds(half * BLK, BLK), :]
        grad_ref[block, :, 0] = dk.astype(jnp.bfloat16).reshape(2, BLK // 2, HD)
        grad_ref[block, :, 1] = dv.astype(jnp.bfloat16).reshape(2, BLK // 2, HD)

    for j in range(NBL):
        put(info_ref[0, 1] + j, OWNP + j // 2, j % 2)

    def put_pair(p, carry):
        put(info_ref[1, 2 * p], p, 0)

        @pl.when(2 * p + 1 < remote)
        def _():
            put(info_ref[1, 2 * p + 1], p, 1)

        return carry

    lax.fori_loop(0, pairs, put_pair, 0)


def info_of(ancestors):
    first = lax.axis_index("ctx") * NBL
    lists = lax.dynamic_slice_in_dim(ancestors, first, NBL, 0)
    remote = jnp.sum(((lists >= 0) & (lists < first)).astype(jnp.int32), axis=1)
    own = first + jnp.arange(NBL, dtype=jnp.int32)
    flags = jnp.any(lists[:, None, :] == own[None, :, None], axis=2).astype(jnp.int32)
    width = MAXD
    head = jnp.zeros((1, width), jnp.int32).at[0, 0].set(remote[0]).at[0, 1].set(first)
    slots = jnp.maximum(lists[:1], 0)
    rest = jnp.concatenate([remote[:, None], flags, jnp.zeros((NBL, width - 1 - NBL), jnp.int32)], axis=1)
    return jnp.concatenate([head, slots, rest], axis=0)


def body(queries, keys, values, out_grad, ancestors, parents):
    tokens = queries.shape[0]
    groups = keys.shape[1]
    kv = jnp.stack([keys, values]).transpose(2, 0, 1, 3)
    kv = lax.all_to_all(kv, "head", split_axis=0, concat_axis=0, tiled=True)
    own = kv.reshape(NBL, 2, 2, BLK // 2, HD)
    pool = lax.all_gather(own, "ctx", axis=0, tiled=True)
    q = lax.all_to_all(queries.reshape(tokens, -1), "head", split_axis=1, concat_axis=0, tiled=True)
    g = lax.all_to_all(out_grad.reshape(tokens, -1), "head", split_axis=1, concat_axis=0, tiled=True)
    within = tree_reach_t(parents)
    info = info_of(ancestors)
    vmem = pl.BlockSpec(memory_space=pltpu.VMEM)
    smem = pl.BlockSpec(memory_space=pltpu.SMEM)
    o, dq, grad = pl.pallas_call(
        kernel,
        out_shape=(
            jax.ShapeDtypeStruct(q.shape, jnp.bfloat16),
            jax.ShapeDtypeStruct(q.shape, jnp.bfloat16),
            jax.ShapeDtypeStruct(pool.shape, jnp.bfloat16),
        ),
        in_specs=[smem] + [vmem] * 5,
        out_specs=(vmem,) * 3,
        scratch_shapes=[
            pltpu.VMEM((NPAIR, 2 * BLK, HD), jnp.bfloat16),
            pltpu.VMEM((NPAIR, 2 * BLK, HD), jnp.bfloat16),
            pltpu.VMEM((NPAIR, HD, 2 * BLK), jnp.bfloat16),
            pltpu.VMEM((NPAIR, HD, 2 * BLK), jnp.bfloat16),
            pltpu.VMEM((NPAIR, 2 * BLK, QN), jnp.float32),
            pltpu.VMEM((8, 128), jnp.bfloat16),
            pltpu.VMEM((NPAIR, 2 * BLK, HD), jnp.float32),
            pltpu.VMEM((NPAIR, 2 * BLK, HD), jnp.float32),
        ],
        compiler_params=pltpu.CompilerParams(vmem_limit_bytes=56 << 20),
    )(info, q, g, own, pool, within)
    grad = grad.reshape(4, 8, NBL, 2, 2, BLK // 2, HD)
    y_groups = [[y * 8 + z for y in range(4)] for z in range(8)]
    z_groups = [[y * 8 + z for z in range(8)] for y in range(4)]
    grad = lax.psum_scatter(grad, "ctx", scatter_dimension=1, axis_index_groups=z_groups, tiled=False)
    grad = lax.psum_scatter(grad, "ctx", scatter_dimension=0, axis_index_groups=y_groups, tiled=False)
    grad = grad.reshape(groups, 2, BLK // 2, HD)
    grad = lax.all_to_all(grad, "head", split_axis=0, concat_axis=0, tiled=True)
    grad = grad.transpose(1, 2, 0, 3)
    o = lax.all_to_all(o, "head", split_axis=0, concat_axis=1, tiled=True)
    dq = lax.all_to_all(dq, "head", split_axis=0, concat_axis=1, tiled=True)
    shape = queries.shape
    return (o.reshape(shape), dq.reshape(shape), grad[0], grad[1])


def solution(mesh):
    rows = P(("ctx", "head"), None, None)
    return jax.shard_map(
        body,
        mesh=mesh,
        in_specs=(rows, rows, rows, rows, P(), P("ctx", None)),
        out_specs=(rows, rows, rows, rows),
        check_vma=False,
    )
```

```python
import math

import jax
import jax.numpy as jnp
from jax import lax
from jax.experimental import pallas as pl
from jax.experimental.pallas import tpu as pltpu
from jax.sharding import PartitionSpec as P

HD = 128
GROUP = 5
BLK = 128
NBL = 4
MAXD = 16
QN = GROUP * BLK
SCALE = 1.0 / math.sqrt(HD)
LOG2E = 1.0 / math.log(2.0)
NEG = -1e30
NPAIR = MAXD // 2 + NBL // 2
OWNP = MAXD // 2


def tree_reach_t(parents):
    block_width = parents.shape[-1]
    hops = parents[:, None, :] == jnp.arange(block_width, dtype=jnp.int32)[None, :, None]
    eye = jnp.eye(block_width, dtype=jnp.bool_)[None]
    reached = (hops | eye).astype(jnp.bfloat16)
    for _ in range(max(1, (block_width - 1).bit_length())):
        product = jnp.einsum("bts,bsu->btu", reached, reached, preferred_element_type=jnp.float32)
        reached = jnp.minimum(product, 1.0).astype(jnp.bfloat16)
    return reached.astype(jnp.float32)


def dot(a, b, dims):
    return lax.dot_general(a, b, (dims, ((), ())), preferred_element_type=jnp.float32)


def kernel(
    info_ref, q_ref, g_ref, own_ref, row_ref, cross_ref, within_ref,
    o_ref, dq_ref, row_grad_ref, cross_grad_ref,
    k_s, v_s, kt_s, vt_s, s_s, dk_s, dv_s,
):
    row_grad_ref[...] = jnp.zeros_like(row_grad_ref)
    cross_grad_ref[...] = jnp.zeros_like(cross_grad_ref)
    dk_s[...] = jnp.zeros_like(dk_s)
    dv_s[...] = jnp.zeros_like(dv_s)
    remote = info_ref[0, 0]
    pairs = (remote + 1) // 2
    row_first = info_ref[0, 2]
    crossing = info_ref[0, 3]

    def take(p, half, kv):
        k = kv[:, 0].reshape(BLK, HD)
        v = kv[:, 1].reshape(BLK, HD)
        k_s[p, half * BLK:(half + 1) * BLK, :] = k
        v_s[p, half * BLK:(half + 1) * BLK, :] = v
        kt_s[p, :, half * BLK:(half + 1) * BLK] = k.T
        vt_s[p, :, half * BLK:(half + 1) * BLK] = v.T

    for j in range(NBL):
        take(OWNP + j // 2, j % 2, own_ref[j])

    def load_pair(p, carry):
        for half in range(2):
            slot = 2 * p + half

            @pl.when(slot < crossing)
            def _():
                take(p, half, cross_ref[slot])

            @pl.when(slot >= crossing)
            def _():
                take(p, half, row_ref[jnp.maximum(info_ref[1, slot] - row_first, 0)])

        return carry

    lax.fori_loop(0, pairs, load_pair, 0)

    for i in range(NBL):
        rows = pl.ds(i * BLK, BLK)
        count = info_ref[2 + i, 0]
        my_pairs = (count + 1) // 2
        q = jnp.concatenate([q_ref[rows, r * HD:(r + 1) * HD] for r in range(GROUP)], axis=0)
        g = jnp.concatenate([g_ref[rows, r * HD:(r + 1) * HD] for r in range(GROUP)], axis=0)
        qt = q.T
        gt = g.T
        row_id = lax.broadcasted_iota(jnp.int32, (2 * BLK, 1), 0)

        def fold(x, op):
            y = x.reshape(-1, 8, QN)
            return op(y, axis=0)

        def scores(p, mx):
            raw = dot(k_s[p], qt, ((1,), (0,))) * (SCALE * LOG2E)
            limit = jnp.where(2 * p + 1 < count, 2 * BLK, BLK)
            s = raw + jnp.where(row_id < limit, 0.0, NEG)
            s_s[p] = s
            return jnp.maximum(mx, fold(s, jnp.max))

        mx = lax.fori_loop(0, my_pairs, scores, jnp.full((8, QN), NEG, jnp.float32))
        own_pairs = i // 2 + 1
        for op in range(own_pairs):
            raw = dot(k_s[OWNP + op], qt, ((1,), (0,))) * (SCALE * LOG2E)
            parts = []
            for half in range(2):
                j = 2 * op + half
                piece = raw[half * BLK:(half + 1) * BLK]
                if j < i:
                    piece = piece + jnp.where(info_ref[2 + i, 1 + j] > 0, 0.0, NEG)
                elif j == i:
                    bias = jnp.where(within_ref[i] > 0.5, 0.0, NEG)
                    piece = piece + jnp.concatenate([bias] * GROUP, axis=1)
                else:
                    piece = jnp.full_like(piece, NEG)
                parts.append(piece)
            s = jnp.concatenate(parts, axis=0)
            s_s[OWNP + op] = s
            mx = jnp.maximum(mx, fold(s, jnp.max))
        m = jnp.max(mx, axis=0, keepdims=True)

        def expo(p, total):
            e = jnp.exp2(s_s[p] - m)
            s_s[p] = e
            return total + fold(e, jnp.sum)

        total = lax.fori_loop(0, my_pairs, expo, jnp.zeros((8, QN), jnp.float32))
        for op in range(own_pairs):
            total = expo(OWNP + op, total)
        inv = 1.0 / jnp.sum(total, axis=0, keepdims=True)

        def attend(p, acc):
            prob = s_s[p] * inv
            s_s[p] = prob
            w = prob.astype(jnp.bfloat16)
            dv_s[p] += dot(w, g, ((1,), (0,)))
            return acc + dot(vt_s[p], w, ((1,), (0,)))

        acc = lax.fori_loop(0, my_pairs, attend, jnp.zeros((HD, QN), jnp.float32))
        for op in range(own_pairs):
            acc = attend(OWNP + op, acc)
        ot = acc.astype(jnp.bfloat16)
        delta = jnp.sum(gt.astype(jnp.float32) * ot.astype(jnp.float32), axis=0, keepdims=True)
        for r in range(GROUP):
            o_ref[rows, r * HD:(r + 1) * HD] = ot[:, r * BLK:(r + 1) * BLK].T

        def back(p, acc):
            dprob = dot(v_s[p], gt, ((1,), (0,)))
            ds = (s_s[p] * (dprob - delta)).astype(jnp.bfloat16)
            dk_s[p] += dot(ds, q, ((1,), (0,)))
            return acc + dot(kt_s[p], ds, ((1,), (0,)))

        acc = lax.fori_loop(0, my_pairs, back, jnp.zeros((HD, QN), jnp.float32))
        for op in range(own_pairs):
            acc = back(OWNP + op, acc)
        dqt = (acc * SCALE).astype(jnp.bfloat16)
        for r in range(GROUP):
            dq_ref[rows, r * HD:(r + 1) * HD] = dqt[:, r * BLK:(r + 1) * BLK].T

    def put(out_ref, place, p, half):
        dk = dk_s[p, pl.ds(half * BLK, BLK), :] * SCALE
        dv = dv_s[p, pl.ds(half * BLK, BLK), :]
        out_ref[place, :, 0] = dk.astype(jnp.bfloat16).reshape(2, BLK // 2, HD)
        out_ref[place, :, 1] = dv.astype(jnp.bfloat16).reshape(2, BLK // 2, HD)

    for j in range(NBL):
        put(row_grad_ref, info_ref[0, 1] - row_first + j, OWNP + j // 2, j % 2)

    def put_pair(p, carry):
        for half in range(2):
            slot = 2 * p + half

            @pl.when(slot < crossing)
            def _():
                put(cross_grad_ref, slot, p, half)

            @pl.when((slot >= crossing) & (slot < remote))
            def _():
                put(row_grad_ref, jnp.maximum(info_ref[1, slot] - row_first, 0), p, half)

        return carry

    lax.fori_loop(0, pairs, put_pair, 0)


def pick_kernel(index_ref, from_ref, out_ref):
    out_ref[...] = from_ref[...]


def pick(index, pool):
    count = index.shape[0]
    block = (1,) + pool.shape[1:]
    return pl.pallas_call(
        pick_kernel,
        out_shape=jax.ShapeDtypeStruct((count,) + pool.shape[1:], pool.dtype),
        grid_spec=pltpu.PrefetchScalarGridSpec(
            num_scalar_prefetch=1,
            grid=(count,),
            in_specs=[pl.BlockSpec(block, lambda i, index_ref: (index_ref[i], 0, 0, 0, 0))],
            out_specs=pl.BlockSpec(block, lambda i, index_ref: (i, 0, 0, 0, 0)),
        ),
    )(index, pool)


def merge_kernel(place_ref, valid_ref, row_ref, *rest):
    parts, out_ref = rest[:-1], rest[-1]
    out_ref[...] = row_ref[...]
    for k, part in enumerate(parts):
        for s in range(part.shape[0]):
            at = k * part.shape[0] + s

            @pl.when(valid_ref[at] > 0)
            def _():
                place = place_ref[at]
                both = out_ref[place].astype(jnp.float32) + part[s].astype(jnp.float32)
                out_ref[place] = both.astype(jnp.bfloat16)


YN = 4
ZN = 8
ROW = ZN * NBL
SLOTS = MAXD // ZN
Z_GROUPS = [[y * ZN + z for z in range(ZN)] for y in range(YN)]


def up(x, k):
    pairs = [(y * ZN + z, (y + k) * ZN + z) for y in range(YN - k) for z in range(ZN)]
    return lax.ppermute(x, "ctx", pairs)


def down(x, k):
    pairs = [((y + k) * ZN + z, y * ZN + z) for y in range(YN - k) for z in range(ZN)]
    return lax.ppermute(x, "ctx", pairs)


def info_of(ancestors, c, y):
    first = c * NBL
    row_first = y * ROW
    lists = lax.dynamic_slice_in_dim(ancestors, first, NBL, 0)
    remote = jnp.sum(((lists >= 0) & (lists < first)).astype(jnp.int32), axis=1)
    crossing = jnp.sum(((lists[0] >= 0) & (lists[0] < row_first)).astype(jnp.int32))
    own = first + jnp.arange(NBL, dtype=jnp.int32)
    flags = jnp.any(lists[:, None, :] == own[None, :, None], axis=2).astype(jnp.int32)
    head = jnp.concatenate(
        [jnp.stack([remote[0], first, row_first, crossing]), jnp.zeros((MAXD - 4,), jnp.int32)]
    )[None]
    rest = jnp.concatenate([remote[:, None], flags, jnp.zeros((NBL, MAXD - 1 - NBL), jnp.int32)], axis=1)
    return jnp.concatenate([head, lists[:1], rest], axis=0)


def body(queries, keys, values, out_grad, ancestors, parents):
    tokens = queries.shape[0]
    groups = keys.shape[1]
    c = lax.axis_index("ctx")
    y = c // ZN
    z = c % ZN
    row_lists = ancestors[::ROW]
    slots = lax.dynamic_slice_in_dim(row_lists, z * SLOTS, SLOTS, 1)
    slot_rows = jnp.where(slots >= 0, slots // ROW, -1)
    my_rows = lax.dynamic_index_in_dim(slot_rows, y, 0, keepdims=False)

    kv = jnp.stack([keys, values]).transpose(2, 0, 1, 3)
    kv = lax.all_to_all(kv, "head", split_axis=0, concat_axis=0, tiled=True)
    own = kv.reshape(NBL, 2, 2, BLK // 2, HD)
    row = lax.all_gather(own, "ctx", axis=0, axis_index_groups=Z_GROUPS, tiled=True)
    q = lax.all_to_all(queries.reshape(tokens, -1), "head", split_axis=1, concat_axis=0, tiled=True)
    g = lax.all_to_all(out_grad.reshape(tokens, -1), "head", split_axis=1, concat_axis=0, tiled=True)

    wanted = jnp.clip(slots[1:] - y * ROW, 0, ROW - 1).reshape(-1)
    sent = pick(wanted, row).reshape((YN - 1, SLOTS) + own.shape[1:])
    mine = jnp.zeros((SLOTS,) + own.shape[1:], own.dtype)
    for k in range(1, YN):
        part = lax.dynamic_index_in_dim(sent, jnp.clip(y + k - 1, 0, YN - 2), 0, keepdims=False)
        here = (my_rows == y - k)[:, None, None, None, None]
        mine = jnp.where(here, up(part, k), mine)
    cross = lax.all_gather(mine, "ctx", axis=0, axis_index_groups=Z_GROUPS, tiled=True)

    within = tree_reach_t(parents)
    info = info_of(ancestors, c, y)
    vmem = pl.BlockSpec(memory_space=pltpu.VMEM)
    smem = pl.BlockSpec(memory_space=pltpu.SMEM)
    o, dq, row_grad, cross_grad = pl.pallas_call(
        kernel,
        out_shape=(
            jax.ShapeDtypeStruct(q.shape, jnp.bfloat16),
            jax.ShapeDtypeStruct(q.shape, jnp.bfloat16),
            jax.ShapeDtypeStruct(row.shape, jnp.bfloat16),
            jax.ShapeDtypeStruct(cross.shape, jnp.bfloat16),
        ),
        in_specs=[smem] + [vmem] * 6,
        out_specs=(vmem,) * 4,
        scratch_shapes=[
            pltpu.VMEM((NPAIR, 2 * BLK, HD), jnp.bfloat16),
            pltpu.VMEM((NPAIR, 2 * BLK, HD), jnp.bfloat16),
            pltpu.VMEM((NPAIR, HD, 2 * BLK), jnp.bfloat16),
            pltpu.VMEM((NPAIR, HD, 2 * BLK), jnp.bfloat16),
            pltpu.VMEM((NPAIR, 2 * BLK, QN), jnp.float32),
            pltpu.VMEM((NPAIR, 2 * BLK, HD), jnp.float32),
            pltpu.VMEM((NPAIR, 2 * BLK, HD), jnp.float32),
        ],
        compiler_params=pltpu.CompilerParams(vmem_limit_bytes=56 << 20),
    )(info, q, g, own, row, cross, within)

    cross_grad = lax.psum_scatter(
        cross_grad, "ctx", scatter_dimension=0, axis_index_groups=Z_GROUPS, tiled=True
    )
    o = lax.all_to_all(o, "head", split_axis=0, concat_axis=1, tiled=True)
    dq = lax.all_to_all(dq, "head", split_axis=0, concat_axis=1, tiled=True)
    cross_grad, o, dq = lax.optimization_barrier((cross_grad, o, dq))
    places, valids, parts = [], [], []
    for k in range(1, YN):
        parts.append(down(cross_grad, k))
        above = jnp.minimum(y + k, YN - 1)
        theirs = lax.dynamic_index_in_dim(slots, above, 0, keepdims=False)
        valid = (theirs >= 0) & (theirs // ROW == y) & (y + k < YN)
        places.append(jnp.where(valid, theirs - y * ROW, 0))
        valids.append(valid.astype(jnp.int32))
    row_grad = pl.pallas_call(
        merge_kernel,
        out_shape=jax.ShapeDtypeStruct(row_grad.shape, row_grad.dtype),
        in_specs=[smem, smem] + [vmem] * YN,
        out_specs=vmem,
        compiler_params=pltpu.CompilerParams(vmem_limit_bytes=24 << 20),
    )(jnp.concatenate(places), jnp.concatenate(valids), row_grad, *parts)
    grad = lax.psum_scatter(
        row_grad, "ctx", scatter_dimension=0, axis_index_groups=Z_GROUPS, tiled=True
    )
    grad = grad.reshape(groups, 2, BLK // 2, HD)
    grad = lax.all_to_all(grad, "head", split_axis=0, concat_axis=0, tiled=True)
    grad = grad.transpose(1, 2, 0, 3)
    shape = queries.shape
    return (o.reshape(shape), dq.reshape(shape), grad[0], grad[1])


def solution(mesh):
    rows = P(("ctx", "head"), None, None)
    return jax.shard_map(
        body,
        mesh=mesh,
        in_specs=(rows, rows, rows, rows, P(), P("ctx", None)),
        out_specs=(rows, rows, rows, rows),
        check_vma=False,
    )
```

```python
import math

import jax
import jax.numpy as jnp
from jax import lax
from jax.experimental import pallas as pl
from jax.experimental.pallas import tpu as pltpu
from jax.sharding import PartitionSpec as P

HD = 128
GROUP = 5
BLK = 128
NBL = 4
MAXD = 16
QN = GROUP * BLK
SCALE = 1.0 / math.sqrt(HD)
LOG2E = 1.0 / math.log(2.0)
NEG = -1e30
NPAIR = MAXD // 2 + NBL // 2
OWNP = MAXD // 2


def tree_reach_t(parents):
    block_width = parents.shape[-1]
    hops = parents[:, None, :] == jnp.arange(block_width, dtype=jnp.int32)[None, :, None]
    eye = jnp.eye(block_width, dtype=jnp.bool_)[None]
    reached = (hops | eye).astype(jnp.bfloat16)
    for _ in range(max(1, (block_width - 1).bit_length())):
        product = jnp.einsum("bts,bsu->btu", reached, reached, preferred_element_type=jnp.float32)
        reached = jnp.minimum(product, 1.0).astype(jnp.bfloat16)
    return reached.astype(jnp.float32)


def dot(a, b, dims):
    return lax.dot_general(a, b, (dims, ((), ())), preferred_element_type=jnp.float32)


def kernel(
    info_ref, q_ref, g_ref, own_ref, row_ref, mine_ref, next_ref, last_ref, far_ref, near_ref, within_ref,
    o_ref, dq_ref, row_grad_ref, mine_grad_ref, next_grad_ref, last_grad_ref, far_grad_ref, near_grad_ref,
    k_s, v_s, kt_s, vt_s, s_s, dk_s, dv_s, acc_s, cross_s, cross_grad_s,
):
    row_grad_ref[...] = jnp.zeros_like(row_grad_ref)
    cross_grad_s[...] = jnp.zeros_like(cross_grad_s)
    at = 0
    for ref in (mine_ref, next_ref, last_ref, far_ref, near_ref):
        cross_s[at:at + ref.shape[0]] = ref[...]
        at += ref.shape[0]
    dk_s[...] = jnp.zeros_like(dk_s)
    dv_s[...] = jnp.zeros_like(dv_s)
    remote = info_ref[0, 0]
    pairs = (remote + 1) // 2
    row_first = info_ref[0, 2]
    crossing = info_ref[0, 3]

    def place_of(slot):
        return info_ref[6, slot]


    def take(p, half, kv):
        k = kv[:, 0].reshape(BLK, HD)
        v = kv[:, 1].reshape(BLK, HD)
        k_s[p, half * BLK:(half + 1) * BLK, :] = k
        v_s[p, half * BLK:(half + 1) * BLK, :] = v
        kt_s[p, :, half * BLK:(half + 1) * BLK] = k.T
        vt_s[p, :, half * BLK:(half + 1) * BLK] = v.T

    for j in range(NBL):
        take(OWNP + j // 2, j % 2, own_ref[j])

    def load_pair(p, carry):
        for half in range(2):
            slot = 2 * p + half

            @pl.when(slot < crossing)
            def _():
                take(p, half, cross_s[place_of(slot)])

            @pl.when(slot >= crossing)
            def _():
                take(p, half, row_ref[jnp.maximum(info_ref[1, slot] - row_first, 0)])

        return carry

    lax.fori_loop(0, pairs, load_pair, 0)

    row_id = lax.broadcasted_iota(jnp.int32, (2 * BLK, 1), 0)
    wide = 2 * QN

    def fold(x, op):
        return op(x.reshape(-1, 8, x.shape[-1]), axis=0)

    for u in range(NBL // 2):
        lo, hi = 2 * u, 2 * u + 1
        first, second = info_ref[2 + lo, 0], info_ref[2 + hi, 0]
        my_pairs = (first + 1) // 2
        spans = [(i, r) for i in (lo, hi) for r in range(GROUP)]

        def gather(ref):
            return jnp.concatenate(
                [ref[i * BLK:(i + 1) * BLK, r * HD:(r + 1) * HD] for i, r in spans], axis=0
            )

        q = gather(q_ref)
        g = gather(g_ref)
        qt = q.T
        gt = g.T

        def scores(p, mx):
            raw = dot(k_s[p], qt, ((1,), (0,))) * (SCALE * LOG2E)
            bias = [jnp.where(row_id + 2 * BLK * p < BLK * n, 0.0, NEG) for n in (first, second)]
            s = jnp.concatenate([raw[:, :QN] + bias[0], raw[:, QN:] + bias[1]], axis=1)
            s_s[p] = s
            return jnp.maximum(mx, fold(s, jnp.max))

        mx = lax.fori_loop(0, my_pairs, scores, jnp.full((8, wide), NEG, jnp.float32))
        for op in range(u + 1):
            raw = dot(k_s[OWNP + op], qt, ((1,), (0,))) * (SCALE * LOG2E)
            parts = []
            for half in range(2):
                j = 2 * op + half
                pieces = []
                for at, i in enumerate((lo, hi)):
                    piece = raw[half * BLK:(half + 1) * BLK, at * QN:(at + 1) * QN]
                    if j < i:
                        piece = piece + jnp.where(info_ref[2 + i, 1 + j] > 0, 0.0, NEG)
                    elif j == i:
                        bias = jnp.where(within_ref[i] > 0.5, 0.0, NEG)
                        piece = piece + jnp.concatenate([bias] * GROUP, axis=1)
                    else:
                        piece = jnp.full_like(piece, NEG)
                    pieces.append(piece)
                parts.append(jnp.concatenate(pieces, axis=1))
            s = jnp.concatenate(parts, axis=0)
            s_s[OWNP + op] = s
            mx = jnp.maximum(mx, fold(s, jnp.max))
        m = jnp.max(mx, axis=0, keepdims=True)

        def expo(p, total):
            e = jnp.exp2(s_s[p] - m)
            s_s[p] = e
            return total + fold(e, jnp.sum)

        total = lax.fori_loop(0, my_pairs, expo, jnp.zeros((8, wide), jnp.float32))
        for op in range(u + 1):
            total = expo(OWNP + op, total)
        inv = 1.0 / jnp.sum(total, axis=0, keepdims=True)

        def attend(p, acc):
            prob = s_s[p] * inv
            s_s[p] = prob
            w = prob.astype(jnp.bfloat16)
            dv_s[p] += dot(w, g, ((1,), (0,)))
            acc_s[...] += dot(vt_s[p], w, ((1,), (0,)))
            return acc

        acc_s[...] = jnp.zeros_like(acc_s)
        lax.fori_loop(0, my_pairs, attend, 0)
        for op in range(u + 1):
            attend(OWNP + op, 0)
        acc = acc_s[...]
        ot = acc.astype(jnp.bfloat16)
        delta = jnp.sum(gt.astype(jnp.float32) * ot.astype(jnp.float32), axis=0, keepdims=True)
        for at, (i, r) in enumerate(spans):
            o_ref[i * BLK:(i + 1) * BLK, r * HD:(r + 1) * HD] = ot[:, at * BLK:(at + 1) * BLK].T

        def back(p, acc):
            dprob = dot(v_s[p], gt, ((1,), (0,)))
            ds = (s_s[p] * (dprob - delta)).astype(jnp.bfloat16)
            dk_s[p] += dot(ds, q, ((1,), (0,)))
            acc_s[...] += dot(kt_s[p], ds, ((1,), (0,)))
            return acc

        acc_s[...] = jnp.zeros_like(acc_s)
        lax.fori_loop(0, my_pairs, back, 0)
        for op in range(u + 1):
            back(OWNP + op, 0)
        acc = acc_s[...]
        dqt = (acc * SCALE).astype(jnp.bfloat16)
        for at, (i, r) in enumerate(spans):
            dq_ref[i * BLK:(i + 1) * BLK, r * HD:(r + 1) * HD] = dqt[:, at * BLK:(at + 1) * BLK].T

    def put(out_ref, place, p, half):
        dk = dk_s[p, pl.ds(half * BLK, BLK), :] * SCALE
        dv = dv_s[p, pl.ds(half * BLK, BLK), :]
        out_ref[place, :, 0] = dk.astype(jnp.bfloat16).reshape(2, BLK // 2, HD)
        out_ref[place, :, 1] = dv.astype(jnp.bfloat16).reshape(2, BLK // 2, HD)

    for j in range(NBL):
        put(row_grad_ref, info_ref[0, 1] - row_first + j, OWNP + j // 2, j % 2)

    def put_pair(p, carry):
        for half in range(2):
            slot = 2 * p + half

            @pl.when(slot < crossing)
            def _():
                put(cross_grad_s, place_of(slot), p, half)

            @pl.when((slot >= crossing) & (slot < remote))
            def _():
                put(row_grad_ref, jnp.maximum(info_ref[1, slot] - row_first, 0), p, half)

        return carry

    lax.fori_loop(0, pairs, put_pair, 0)
    at = 0
    for ref in (mine_grad_ref, next_grad_ref, last_grad_ref, far_grad_ref, near_grad_ref):
        ref[...] = cross_grad_s[at:at + ref.shape[0]]
        at += ref.shape[0]


def attention(info, q, g, own, row, cross, within):
    vmem = pl.BlockSpec(memory_space=pltpu.VMEM)
    smem = pl.BlockSpec(memory_space=pltpu.SMEM)
    like = [jax.ShapeDtypeStruct(a.shape, jnp.bfloat16) for a in (q, q, row, *cross)]
    return pl.pallas_call(
        kernel,
        out_shape=tuple(like),
        in_specs=[smem] + [vmem] * (5 + len(cross)),
        out_specs=(vmem,) * len(like),
        scratch_shapes=[
            pltpu.VMEM((NPAIR, 2 * BLK, HD), jnp.bfloat16),
            pltpu.VMEM((NPAIR, 2 * BLK, HD), jnp.bfloat16),
            pltpu.VMEM((NPAIR, HD, 2 * BLK), jnp.bfloat16),
            pltpu.VMEM((NPAIR, HD, 2 * BLK), jnp.bfloat16),
            pltpu.VMEM((NPAIR, 2 * BLK, 2 * QN), jnp.float32),
            pltpu.VMEM((NPAIR, 2 * BLK, HD), jnp.float32),
            pltpu.VMEM((NPAIR, 2 * BLK, HD), jnp.float32),
            pltpu.VMEM((HD, 2 * QN), jnp.float32),
            pltpu.VMEM((MAXD,) + own.shape[1:], jnp.bfloat16),
            pltpu.VMEM((MAXD,) + own.shape[1:], jnp.bfloat16),
        ],
        compiler_params=pltpu.CompilerParams(vmem_limit_bytes=56 << 20),
    )(info, q, g, own, row, *cross, within)


def pick_kernel(index_ref, from_ref, *outs):
    for k, out in enumerate(outs):
        for s in range(out.shape[0]):
            out[s] = from_ref[index_ref[k * out.shape[0] + s]]


def pick(index, pool, parts):
    vmem = pl.BlockSpec(memory_space=pltpu.VMEM)
    size = index.shape[0] // parts
    return pl.pallas_call(
        pick_kernel,
        out_shape=(jax.ShapeDtypeStruct((size,) + pool.shape[1:], pool.dtype),) * parts,
        in_specs=[pl.BlockSpec(memory_space=pltpu.SMEM), vmem],
        out_specs=(vmem,) * parts,
        compiler_params=pltpu.CompilerParams(vmem_limit_bytes=24 << 20),
    )(index, pool)


def merge_kernel(place_ref, valid_ref, row_ref, *rest):
    parts, out_ref = rest[:-1], rest[-1]
    out_ref[...] = row_ref[...]
    for k, part in enumerate(parts):
        for s in range(part.shape[0]):
            at = k * part.shape[0] + s

            @pl.when(valid_ref[at] > 0)
            def _():
                place = place_ref[at]
                both = out_ref[place].astype(jnp.float32) + part[s].astype(jnp.float32)
                out_ref[place] = both.astype(jnp.bfloat16)


YN = 4
ZN = 8
ROW = ZN * NBL
SETS = 4
SLOTS = MAXD // SETS
Z_GROUPS = [[y * ZN + z for z in range(ZN)] for y in range(YN)]


def along(x, k):
    pairs = [(y * ZN + z, y * ZN + (z + k) % ZN) for y in range(YN) for z in range(ZN)]
    return lax.ppermute(x, "ctx", pairs)


def up(x, k):
    pairs = [(y * ZN + z, (y + k) * ZN + z) for y in range(YN - k) for z in range(ZN)]
    return lax.ppermute(x, "ctx", pairs)


def down(x, k):
    pairs = [((y + k) * ZN + z, y * ZN + z) for y in range(YN - k) for z in range(ZN)]
    return lax.ppermute(x, "ctx", pairs)


def info_of(ancestors, c, y, z):
    first = c * NBL
    row_first = y * ROW
    lists = lax.dynamic_slice_in_dim(ancestors, first, NBL, 0)
    remote = jnp.sum(((lists >= 0) & (lists < first)).astype(jnp.int32), axis=1)
    crossing = jnp.sum(((lists[0] >= 0) & (lists[0] < row_first)).astype(jnp.int32))
    own = first + jnp.arange(NBL, dtype=jnp.int32)
    flags = jnp.any(lists[:, None, :] == own[None, :, None], axis=2).astype(jnp.int32)
    head = jnp.concatenate(
        [jnp.stack([remote[0], first, row_first, crossing]), jnp.zeros((MAXD - 4,), jnp.int32)]
    )[None]
    rest = jnp.concatenate([remote[:, None], flags, jnp.zeros((NBL, MAXD - 1 - NBL), jnp.int32)], axis=1)
    slot = jnp.arange(MAXD, dtype=jnp.int32)
    turn = (slot // SLOTS - z) % SETS
    base = jnp.array([0, SLOTS, 3 * SLOTS, 2 * SLOTS], jnp.int32)
    place = (base[turn] + slot % SLOTS)[None]
    return jnp.concatenate([head, lists[:1], rest, place], axis=0)


def body(queries, keys, values, out_grad, ancestors, parents):
    tokens = queries.shape[0]
    groups = keys.shape[1]
    c = lax.axis_index("ctx")
    y = c // ZN
    z = c % ZN
    row_lists = ancestors[::ROW]
    slots = lax.dynamic_slice_in_dim(row_lists, (z % SETS) * SLOTS, SLOTS, 1)
    slot_rows = jnp.where(slots >= 0, slots // ROW, -1)
    my_rows = lax.dynamic_index_in_dim(slot_rows, y, 0, keepdims=False)

    kv = jnp.stack([keys, values]).transpose(2, 0, 1, 3)
    kv = lax.all_to_all(kv, "head", split_axis=0, concat_axis=0, tiled=True)
    own = kv.reshape(NBL, 2, 2, BLK // 2, HD)
    row = lax.all_gather(own, "ctx", axis=0, axis_index_groups=Z_GROUPS, tiled=True)
    q = lax.all_to_all(queries.reshape(tokens, -1), "head", split_axis=1, concat_axis=0, tiled=True)
    g = lax.all_to_all(out_grad.reshape(tokens, -1), "head", split_axis=1, concat_axis=0, tiled=True)

    row, q, g = lax.optimization_barrier((row, q, g))

    def of_row(k):
        return lax.dynamic_index_in_dim(slots, jnp.minimum(y + k, YN - 1), 0, keepdims=False)

    wanted = [jnp.clip(of_row(k) - y * ROW, 0, ROW - 1) for k in range(1, YN)]
    sent = pick(jnp.concatenate(wanted), row, YN - 1)
    mine = jnp.zeros((SLOTS,) + own.shape[1:], own.dtype)
    for k in range(1, YN):
        here = (my_rows == y - k)[:, None, None, None, None]
        mine = jnp.where(here, up(sent[k - 1], k), mine)
    half = SLOTS // 2
    cross = (mine, along(mine, -1), along(mine, 1), along(mine[:half], -2), along(mine[half:], 2))

    within = tree_reach_t(parents)
    info = info_of(ancestors, c, y, z)
    o, dq, row_grad, *turns = attention(info, q, g, own, row, cross, within)

    here = turns[0].astype(jnp.float32)
    here = here + along(turns[1], 1).astype(jnp.float32) + along(turns[2], -1).astype(jnp.float32)
    far = jnp.concatenate([along(turns[3], 2), along(turns[4], -2)], axis=0)
    here = (here + far.astype(jnp.float32)).astype(jnp.bfloat16)
    places, valids, parts = [], [], []
    for k in range(1, YN):
        parts.append(down(here, k))
        theirs = of_row(k)
        valid = (theirs >= 0) & (theirs // ROW == y) & (y + k < YN)
        places.append(jnp.where(valid, theirs - y * ROW, 0))
        valids.append(valid.astype(jnp.int32))
    vmem = pl.BlockSpec(memory_space=pltpu.VMEM)
    smem = pl.BlockSpec(memory_space=pltpu.SMEM)
    row_grad = pl.pallas_call(
        merge_kernel,
        out_shape=jax.ShapeDtypeStruct(row_grad.shape, row_grad.dtype),
        in_specs=[smem, smem] + [vmem] * YN,
        out_specs=vmem,
        compiler_params=pltpu.CompilerParams(vmem_limit_bytes=24 << 20),
    )(jnp.concatenate(places), jnp.concatenate(valids), row_grad, *parts)
    row_grad, o, dq = lax.optimization_barrier((row_grad, o, dq))
    grad = lax.psum_scatter(
        row_grad, "ctx", scatter_dimension=0, axis_index_groups=Z_GROUPS, tiled=True
    )
    o = lax.all_to_all(o, "head", split_axis=0, concat_axis=1, tiled=True)
    dq = lax.all_to_all(dq, "head", split_axis=0, concat_axis=1, tiled=True)
    grad, o, dq = lax.optimization_barrier((grad, o, dq))
    grad = grad.reshape(groups, 2, BLK // 2, HD)
    grad = lax.all_to_all(grad, "head", split_axis=0, concat_axis=0, tiled=True)
    grad = grad.transpose(1, 2, 0, 3)
    shape = queries.shape
    return (o.reshape(shape), dq.reshape(shape), grad[0], grad[1])


def solution(mesh):
    rows = P(("ctx", "head"), None, None)
    return jax.shard_map(
        body,
        mesh=mesh,
        in_specs=(rows, rows, rows, rows, P(), P("ctx", None)),
        out_specs=(rows, rows, rows, rows),
        check_vma=False,
    )
```

```python
import math

import jax
import jax.numpy as jnp
from jax import lax
from jax.experimental import pallas as pl
from jax.experimental.pallas import tpu as pltpu
from jax.sharding import PartitionSpec as P

HD = 128
GROUP = 5
BLK = 128
NBL = 4
MAXD = 16
QN = GROUP * BLK
SCALE = 1.0 / math.sqrt(HD)
LOG2E = 1.0 / math.log(2.0)
NEG = -1e30
OWNP = NBL // 2
NPAIR = OWNP + MAXD // 2 + 1
WIDE = NBL * QN


def tree_reach_t(parents):
    block_width = parents.shape[-1]
    hops = parents[:, None, :] == jnp.arange(block_width, dtype=jnp.int32)[None, :, None]
    eye = jnp.eye(block_width, dtype=jnp.bool_)[None]
    reached = (hops | eye).astype(jnp.bfloat16)
    for _ in range(max(1, (block_width - 1).bit_length())):
        product = jnp.einsum("bts,bsu->btu", reached, reached, preferred_element_type=jnp.float32)
        reached = jnp.minimum(product, 1.0).astype(jnp.bfloat16)
    return reached.astype(jnp.float32)


def dot(a, b, dims):
    return lax.dot_general(a, b, (dims, ((), ())), preferred_element_type=jnp.float32)


def gather(ref):
    return jnp.concatenate(
        [ref[i * BLK:(i + 1) * BLK, r * HD:(r + 1) * HD] for i in range(NBL) for r in range(GROUP)],
        axis=0,
    )


def fold(x, op):
    return op(x.reshape(-1, 8, x.shape[-1]), axis=0)


def limits(counts, p):
    row_id = lax.broadcasted_iota(jnp.int32, (2 * BLK, 1), 0)
    return [jnp.where(row_id + 2 * BLK * p < BLK * n, 0.0, NEG) for n in counts]


def masked(raw, bias):
    return jnp.concatenate([raw[:, i * QN:(i + 1) * QN] + bias[i] for i in range(NBL)], axis=1)


def own_kernel(
    info_ref, q_ref, g_ref, own_ref, within_ref,
    q_out, g_out, qt_out, gt_out, e_ref, max_ref, sum_ref,
):
    q = gather(q_ref)
    g = gather(g_ref)
    qt = q.T
    q_out[...] = q
    g_out[...] = g
    qt_out[...] = qt
    gt_out[...] = g.T
    mx = jnp.full((8, WIDE), NEG, jnp.float32)
    for p in range(OWNP):
        k = own_ref[2 * p:2 * p + 2, :, 0].reshape(2 * BLK, HD)
        raw = dot(k, qt, ((1,), (0,))) * (SCALE * LOG2E)
        parts = []
        for half in range(2):
            j = 2 * p + half
            pieces = []
            for i in range(NBL):
                piece = raw[half * BLK:(half + 1) * BLK, i * QN:(i + 1) * QN]
                if j < i:
                    piece = piece + jnp.where(info_ref[2 + i, 1 + j] > 0, 0.0, NEG)
                elif j == i:
                    bias = jnp.where(within_ref[i] > 0.5, 0.0, NEG)
                    piece = piece + jnp.concatenate([bias] * GROUP, axis=1)
                else:
                    piece = jnp.full_like(piece, NEG)
                pieces.append(piece)
            parts.append(jnp.concatenate(pieces, axis=1))
        s = jnp.concatenate(parts, axis=0)
        e_ref[p] = s
        mx = jnp.maximum(mx, fold(s, jnp.max))
    m = jnp.max(mx, axis=0, keepdims=True)
    total = jnp.zeros((8, WIDE), jnp.float32)
    for p in range(OWNP):
        e = jnp.exp2(e_ref[p] - m)
        e_ref[p] = e
        total = total + fold(e, jnp.sum)
    max_ref[...] = m
    sum_ref[...] = jnp.sum(total, axis=0, keepdims=True)


def row_kernel(info_ref, qt_ref, row_ref, e_ref, max_ref, sum_ref, s_s, sems):
    remote = info_ref[0, 0]
    row_first = info_ref[0, 2]
    crossing = info_ref[0, 3]
    pairs = (remote - crossing + 1) // 2
    counts = [info_ref[2 + i, 0] - crossing for i in range(NBL)]

    def scores(p, mx):
        ks = []
        for half in range(2):
            block = info_ref[1, jnp.minimum(crossing + 2 * p + half, MAXD - 1)]
            ks.append(row_ref[jnp.maximum(block - row_first, 0), :, 0].reshape(BLK, HD))
        k = jnp.concatenate(ks, axis=0)
        raw = dot(k, qt_ref[...], ((1,), (0,))) * (SCALE * LOG2E)
        s = masked(raw, limits(counts, p))
        s_s[p] = s
        return jnp.maximum(mx, fold(s, jnp.max))

    mx = lax.fori_loop(0, pairs, scores, jnp.full((8, WIDE), NEG, jnp.float32))
    m = jnp.max(mx, axis=0, keepdims=True)

    def expo(p, total):
        e = jnp.exp2(s_s[p] - m)
        s_s[p] = e
        pltpu.make_async_copy(s_s.at[p], e_ref.at[p], sems.at[p]).start()
        return total + fold(e, jnp.sum)

    total = lax.fori_loop(0, pairs, expo, jnp.zeros((8, WIDE), jnp.float32))
    max_ref[...] = m
    sum_ref[...] = jnp.sum(total, axis=0, keepdims=True)

    def finish(p, carry):
        pltpu.make_async_copy(s_s.at[p], e_ref.at[p], sems.at[p]).wait()
        return carry

    lax.fori_loop(0, pairs, finish, 0)


def kernel(
    info_ref, q_ref, g_ref, qt_ref, gt_ref, own_ref, row_ref,
    mine_ref, next_ref, last_ref, far_ref, near_ref,
    own_max, own_sum, row_max, row_sum, own_e, row_e,
    o_ref, dq_ref, row_grad_ref, mine_grad_ref, next_grad_ref, last_grad_ref, far_grad_ref, near_grad_ref,
    k_s, v_s, kt_s, vt_s, s_s, dk_s, dv_s, acc_s, fac_s, cross_s, cross_grad_s, sems,
):
    remote = info_ref[0, 0]
    row_first = info_ref[0, 2]
    crossing = info_ref[0, 3]
    row_pairs = (remote - crossing + 1) // 2
    cross_pairs = (crossing + 1) // 2
    cross_at = OWNP + row_pairs
    pairs = cross_at + cross_pairs

    def own_copy(p):
        return pltpu.make_async_copy(own_e.at[p], s_s.at[p], sems.at[p])

    def row_copy(p):
        return pltpu.make_async_copy(row_e.at[p], s_s.at[OWNP + p], sems.at[OWNP + p])

    for p in range(OWNP):
        own_copy(p).start()

    def begin(p, carry):
        row_copy(p).start()
        return carry

    lax.fori_loop(0, row_pairs, begin, 0)

    row_grad_ref[...] = jnp.zeros_like(row_grad_ref)
    cross_grad_s[...] = jnp.zeros_like(cross_grad_s)
    at = 0
    for ref in (mine_ref, next_ref, last_ref, far_ref, near_ref):
        cross_s[at:at + ref.shape[0]] = ref[...]
        at += ref.shape[0]

    def row_place(slot):
        return jnp.maximum(info_ref[1, jnp.minimum(slot, MAXD - 1)] - row_first, 0)

    def take(p, half, kv):
        k = kv[:, 0].reshape(BLK, HD)
        v = kv[:, 1].reshape(BLK, HD)
        k_s[p, half * BLK:(half + 1) * BLK, :] = k
        v_s[p, half * BLK:(half + 1) * BLK, :] = v
        kt_s[p, :, half * BLK:(half + 1) * BLK] = k.T
        vt_s[p, :, half * BLK:(half + 1) * BLK] = v.T

    for j in range(NBL):
        take(j // 2, j % 2, own_ref[j])

    def load_row(p, carry):
        for half in range(2):
            take(OWNP + p, half, row_ref[row_place(crossing + 2 * p + half)])
        return carry

    lax.fori_loop(0, row_pairs, load_row, 0)

    def load_cross(p, carry):
        for half in range(2):
            take(cross_at + p, half, cross_s[info_ref[6, 2 * p + half]])
        return carry

    lax.fori_loop(0, cross_pairs, load_cross, 0)

    counts = [jnp.minimum(info_ref[2 + i, 0], crossing) for i in range(NBL)]

    def scores(p, mx):
        raw = dot(k_s[cross_at + p], qt_ref[...], ((1,), (0,))) * (SCALE * LOG2E)
        s = masked(raw, limits(counts, p))
        s_s[cross_at + p] = s
        return jnp.maximum(mx, fold(s, jnp.max))

    mx = lax.fori_loop(0, cross_pairs, scores, jnp.full((8, WIDE), NEG, jnp.float32))
    m = jnp.max(mx, axis=0, keepdims=True)
    m = jnp.maximum(m, jnp.maximum(own_max[...], row_max[...]))

    def expo(p, total):
        e = jnp.exp2(s_s[cross_at + p] - m)
        s_s[cross_at + p] = e
        return total + fold(e, jnp.sum)

    total = lax.fori_loop(0, cross_pairs, expo, jnp.zeros((8, WIDE), jnp.float32))
    own_f = jnp.exp2(own_max[...] - m)
    row_f = jnp.exp2(row_max[...] - m)
    total = jnp.sum(total, axis=0, keepdims=True) + own_sum[...] * own_f + row_sum[...] * row_f
    inv = 1.0 / total
    fac_s[0] = own_f * inv
    fac_s[1] = row_f * inv
    fac_s[2] = inv

    acc_s[...] = jnp.zeros_like(acc_s)

    def attend(p, carry):
        @pl.when(p < cross_at)
        def _():
            pltpu.make_async_copy(own_e.at[0], s_s.at[p], sems.at[p]).wait()

        kind = jnp.where(p < OWNP, 0, jnp.where(p < cross_at, 1, 2))
        prob = s_s[p] * fac_s[kind]
        s_s[p] = prob
        w = prob.astype(jnp.bfloat16)
        dv_s[p] = dot(w, g_ref[...], ((1,), (0,)))
        acc_s[...] += dot(vt_s[p], w, ((1,), (0,)))
        return carry

    lax.fori_loop(0, pairs, attend, 0)
    ot = acc_s[...].astype(jnp.bfloat16)
    delta = jnp.sum(
        gt_ref[...].astype(jnp.float32) * ot.astype(jnp.float32), axis=0, keepdims=True
    )

    def spread(ref, x):
        for i in range(NBL):
            for r in range(GROUP):
                at = (i * GROUP + r) * BLK
                ref[i * BLK:(i + 1) * BLK, r * HD:(r + 1) * HD] = x[:, at:at + BLK].T

    spread(o_ref, ot)
    acc_s[...] = jnp.zeros_like(acc_s)

    def back(p, carry):
        dprob = dot(v_s[p], gt_ref[...], ((1,), (0,)))
        ds = (s_s[p] * (dprob - delta)).astype(jnp.bfloat16)
        dk_s[p] = dot(ds, q_ref[...], ((1,), (0,)))
        acc_s[...] += dot(kt_s[p], ds, ((1,), (0,)))
        return carry

    lax.fori_loop(0, pairs, back, 0)
    spread(dq_ref, (acc_s[...] * SCALE).astype(jnp.bfloat16))

    def put(out_ref, place, p, half):
        dk = dk_s[p, pl.ds(half * BLK, BLK), :] * SCALE
        dv = dv_s[p, pl.ds(half * BLK, BLK), :]
        out_ref[place, :, 0] = dk.astype(jnp.bfloat16).reshape(2, BLK // 2, HD)
        out_ref[place, :, 1] = dv.astype(jnp.bfloat16).reshape(2, BLK // 2, HD)

    for j in range(NBL):
        put(row_grad_ref, info_ref[0, 1] - row_first + j, j // 2, j % 2)

    def put_row(p, carry):
        for half in range(2):
            slot = crossing + 2 * p + half

            @pl.when(slot < remote)
            def _():
                put(row_grad_ref, row_place(slot), OWNP + p, half)

        return carry

    lax.fori_loop(0, row_pairs, put_row, 0)

    def put_cross(p, carry):
        for half in range(2):
            slot = 2 * p + half

            @pl.when(slot < crossing)
            def _():
                put(cross_grad_s, info_ref[6, slot], cross_at + p, half)

        return carry

    lax.fori_loop(0, cross_pairs, put_cross, 0)
    at = 0
    for ref in (mine_grad_ref, next_grad_ref, last_grad_ref, far_grad_ref, near_grad_ref):
        ref[...] = cross_grad_s[at:at + ref.shape[0]]
        at += ref.shape[0]


VM = pl.BlockSpec(memory_space=pltpu.VMEM)
SM = pl.BlockSpec(memory_space=pltpu.SMEM)
ANY = pl.BlockSpec(memory_space=pl.ANY)
LIMIT = pltpu.CompilerParams(vmem_limit_bytes=58 << 20)


def like(shape, dtype=jnp.bfloat16):
    return jax.ShapeDtypeStruct(shape, dtype)


def own_part(info, q, g, own, within):
    line = like((1, WIDE), jnp.float32)
    return pl.pallas_call(
        own_kernel,
        out_shape=(
            like((WIDE, HD)), like((WIDE, HD)), like((HD, WIDE)), like((HD, WIDE)),
            like((OWNP, 2 * BLK, WIDE), jnp.float32), line, line,
        ),
        in_specs=[SM] + [VM] * 4,
        out_specs=(VM,) * 7,
        compiler_params=LIMIT,
    )(info, q, g, own, within)


def row_part(info, qt, row):
    line = like((1, WIDE), jnp.float32)
    tiles = (MAXD // 2, 2 * BLK, WIDE)
    return pl.pallas_call(
        row_kernel,
        out_shape=(like(tiles, jnp.float32), line, line),
        in_specs=[SM, VM, VM],
        out_specs=(ANY, VM, VM),
        scratch_shapes=[pltpu.VMEM(tiles, jnp.float32), pltpu.SemaphoreType.DMA((MAXD // 2,))],
        compiler_params=LIMIT,
    )(info, qt, row)


def last_part(info, q, own, row, cross, own_stuff, row_stuff):
    qs, gs, qt, gt, own_e, own_max, own_sum = own_stuff
    row_e, row_max, row_sum = row_stuff
    outs = tuple(like(a.shape) for a in (q, q, row, *cross))
    return pl.pallas_call(
        kernel,
        out_shape=outs,
        in_specs=[SM] + [VM] * (10 + len(cross)) + [ANY] * 2,
        out_specs=(VM,) * len(outs),
        scratch_shapes=[
            pltpu.VMEM((NPAIR, 2 * BLK, HD), jnp.bfloat16),
            pltpu.VMEM((NPAIR, 2 * BLK, HD), jnp.bfloat16),
            pltpu.VMEM((NPAIR, HD, 2 * BLK), jnp.bfloat16),
            pltpu.VMEM((NPAIR, HD, 2 * BLK), jnp.bfloat16),
            pltpu.VMEM((NPAIR, 2 * BLK, WIDE), jnp.float32),
            pltpu.VMEM((NPAIR, 2 * BLK, HD), jnp.float32),
            pltpu.VMEM((NPAIR, 2 * BLK, HD), jnp.float32),
            pltpu.VMEM((HD, WIDE), jnp.float32),
            pltpu.VMEM((3, 1, WIDE), jnp.float32),
            pltpu.VMEM((MAXD,) + own.shape[1:], jnp.bfloat16),
            pltpu.VMEM((MAXD,) + own.shape[1:], jnp.bfloat16),
            pltpu.SemaphoreType.DMA((NPAIR,)),
        ],
        compiler_params=LIMIT,
    )(info, qs, gs, qt, gt, own, row, *cross, own_max, own_sum, row_max, row_sum, own_e, row_e)


def pick_kernel(index_ref, from_ref, *outs):
    for k, out in enumerate(outs):
        for s in range(out.shape[0]):
            out[s] = from_ref[index_ref[k * out.shape[0] + s]]


def pick(index, pool, parts):
    vmem = pl.BlockSpec(memory_space=pltpu.VMEM)
    size = index.shape[0] // parts
    return pl.pallas_call(
        pick_kernel,
        out_shape=(jax.ShapeDtypeStruct((size,) + pool.shape[1:], pool.dtype),) * parts,
        in_specs=[pl.BlockSpec(memory_space=pltpu.SMEM), vmem],
        out_specs=(vmem,) * parts,
        compiler_params=pltpu.CompilerParams(vmem_limit_bytes=24 << 20),
    )(index, pool)


def merge_kernel(place_ref, valid_ref, row_ref, *rest):
    parts, out_ref = rest[:-1], rest[-1]
    out_ref[...] = row_ref[...]
    for k, part in enumerate(parts):
        for s in range(part.shape[0]):
            at = k * part.shape[0] + s

            @pl.when(valid_ref[at] > 0)
            def _():
                place = place_ref[at]
                both = out_ref[place].astype(jnp.float32) + part[s].astype(jnp.float32)
                out_ref[place] = both.astype(jnp.bfloat16)


YN = 4
ZN = 8
ROW = ZN * NBL
SETS = 4
SLOTS = MAXD // SETS
Z_GROUPS = [[y * ZN + z for z in range(ZN)] for y in range(YN)]


def along(x, k):
    pairs = [(y * ZN + z, y * ZN + (z + k) % ZN) for y in range(YN) for z in range(ZN)]
    return lax.ppermute(x, "ctx", pairs)


def up(x, k):
    pairs = [(y * ZN + z, (y + k) * ZN + z) for y in range(YN - k) for z in range(ZN)]
    return lax.ppermute(x, "ctx", pairs)


def down(x, k):
    pairs = [((y + k) * ZN + z, y * ZN + z) for y in range(YN - k) for z in range(ZN)]
    return lax.ppermute(x, "ctx", pairs)


def info_of(ancestors, c, y, z):
    first = c * NBL
    row_first = y * ROW
    lists = lax.dynamic_slice_in_dim(ancestors, first, NBL, 0)
    remote = jnp.sum(((lists >= 0) & (lists < first)).astype(jnp.int32), axis=1)
    crossing = jnp.sum(((lists[0] >= 0) & (lists[0] < row_first)).astype(jnp.int32))
    own = first + jnp.arange(NBL, dtype=jnp.int32)
    flags = jnp.any(lists[:, None, :] == own[None, :, None], axis=2).astype(jnp.int32)
    head = jnp.concatenate(
        [jnp.stack([remote[0], first, row_first, crossing]), jnp.zeros((MAXD - 4,), jnp.int32)]
    )[None]
    rest = jnp.concatenate([remote[:, None], flags, jnp.zeros((NBL, MAXD - 1 - NBL), jnp.int32)], axis=1)
    slot = jnp.arange(MAXD, dtype=jnp.int32)
    turn = (slot // SLOTS - z) % SETS
    base = jnp.array([0, SLOTS, 3 * SLOTS, 2 * SLOTS], jnp.int32)
    place = (base[turn] + slot % SLOTS)[None]
    return jnp.concatenate([head, lists[:1], rest, place], axis=0)


def body(queries, keys, values, out_grad, ancestors, parents):
    tokens = queries.shape[0]
    groups = keys.shape[1]
    c = lax.axis_index("ctx")
    y = c // ZN
    z = c % ZN
    row_lists = ancestors[::ROW]
    slots = lax.dynamic_slice_in_dim(row_lists, (z % SETS) * SLOTS, SLOTS, 1)
    slot_rows = jnp.where(slots >= 0, slots // ROW, -1)
    my_rows = lax.dynamic_index_in_dim(slot_rows, y, 0, keepdims=False)

    kv = jnp.stack([keys, values]).transpose(2, 0, 1, 3)
    kv = lax.all_to_all(kv, "head", split_axis=0, concat_axis=0, tiled=True)
    own = kv.reshape(NBL, 2, 2, BLK // 2, HD)
    row = lax.all_gather(own, "ctx", axis=0, axis_index_groups=Z_GROUPS, tiled=True)
    q = lax.all_to_all(queries.reshape(tokens, -1), "head", split_axis=1, concat_axis=0, tiled=True)
    g = lax.all_to_all(out_grad.reshape(tokens, -1), "head", split_axis=1, concat_axis=0, tiled=True)

    row, q, g = lax.optimization_barrier((row, q, g))

    def of_row(k):
        return lax.dynamic_index_in_dim(slots, jnp.minimum(y + k, YN - 1), 0, keepdims=False)

    within = tree_reach_t(parents)
    info = info_of(ancestors, c, y, z)
    wanted = [jnp.clip(of_row(k) - y * ROW, 0, ROW - 1) for k in range(1, YN)]
    sent = pick(jnp.concatenate(wanted), row, YN - 1)
    sent, q, g = lax.optimization_barrier((sent, q, g))
    moved = [up(sent[k - 1], k) for k in range(1, YN)]
    own_stuff = own_part(info, q, g, own, within)
    moved, own_stuff = lax.optimization_barrier((moved, own_stuff))
    mine = jnp.zeros((SLOTS,) + own.shape[1:], own.dtype)
    for k in range(1, YN):
        here = (my_rows == y - k)[:, None, None, None, None]
        mine = jnp.where(here, moved[k - 1], mine)
    half = SLOTS // 2
    cross = (mine, along(mine, -1), along(mine, 1), along(mine[:half], -2), along(mine[half:], 2))
    row_stuff = row_part(info, own_stuff[2], row)
    o, dq, row_grad, *turns = last_part(info, q, own, row, cross, own_stuff, row_stuff)

    here = turns[0].astype(jnp.float32)
    here = here + along(turns[1], 1).astype(jnp.float32) + along(turns[2], -1).astype(jnp.float32)
    far = jnp.concatenate([along(turns[3], 2), along(turns[4], -2)], axis=0)
    here = (here + far.astype(jnp.float32)).astype(jnp.bfloat16)
    places, valids, parts = [], [], []
    for k in range(1, YN):
        parts.append(down(here, k))
        theirs = of_row(k)
        valid = (theirs >= 0) & (theirs // ROW == y) & (y + k < YN)
        places.append(jnp.where(valid, theirs - y * ROW, 0))
        valids.append(valid.astype(jnp.int32))
    vmem = pl.BlockSpec(memory_space=pltpu.VMEM)
    smem = pl.BlockSpec(memory_space=pltpu.SMEM)
    row_grad = pl.pallas_call(
        merge_kernel,
        out_shape=jax.ShapeDtypeStruct(row_grad.shape, row_grad.dtype),
        in_specs=[smem, smem] + [vmem] * YN,
        out_specs=vmem,
        compiler_params=pltpu.CompilerParams(vmem_limit_bytes=24 << 20),
    )(jnp.concatenate(places), jnp.concatenate(valids), row_grad, *parts)
    row_grad, o, dq = lax.optimization_barrier((row_grad, o, dq))
    grad = lax.psum_scatter(
        row_grad, "ctx", scatter_dimension=0, axis_index_groups=Z_GROUPS, tiled=True
    )
    o = lax.all_to_all(o, "head", split_axis=0, concat_axis=1, tiled=True)
    dq = lax.all_to_all(dq, "head", split_axis=0, concat_axis=1, tiled=True)
    grad, o, dq = lax.optimization_barrier((grad, o, dq))
    grad = grad.reshape(groups, 2, BLK // 2, HD)
    grad = lax.all_to_all(grad, "head", split_axis=0, concat_axis=0, tiled=True)
    grad = grad.transpose(1, 2, 0, 3)
    shape = queries.shape
    return (o.reshape(shape), dq.reshape(shape), grad[0], grad[1])


def solution(mesh):
    rows = P(("ctx", "head"), None, None)
    return jax.shard_map(
        body,
        mesh=mesh,
        in_specs=(rows, rows, rows, rows, P(), P("ctx", None)),
        out_specs=(rows, rows, rows, rows),
        check_vma=False,
    )
```

```python
import functools
import math

import jax
import jax.numpy as jnp
from jax import lax
from jax.experimental import pallas as pl
from jax.experimental.pallas import tpu as pltpu
from jax.sharding import PartitionSpec as P

HD = 128
GROUP = 5
BLK = 128
NBL = 4
MAXD = 16
QN = GROUP * BLK
SCALE = 1.0 / math.sqrt(HD)
LOG2E = 1.0 / math.log(2.0)
NEG = -1e30
OWNP = NBL // 2
NPAIR = OWNP + MAXD // 2 + 1
WIDE = NBL * QN
YN = 4
ZN = 8


def tree_reach_t(parents):
    block_width = parents.shape[-1]
    hops = parents[:, None, :] == jnp.arange(block_width, dtype=jnp.int32)[None, :, None]
    eye = jnp.eye(block_width, dtype=jnp.bool_)[None]
    reached = (hops | eye).astype(jnp.bfloat16)
    for _ in range(max(1, (block_width - 1).bit_length())):
        product = jnp.einsum("bts,bsu->btu", reached, reached, preferred_element_type=jnp.float32)
        reached = jnp.minimum(product, 1.0).astype(jnp.bfloat16)
    return reached.astype(jnp.float32)


def dot(a, b, dims):
    return lax.dot_general(a, b, (dims, ((), ())), preferred_element_type=jnp.float32)


def gather(ref):
    return jnp.concatenate(
        [ref[i * BLK:(i + 1) * BLK, r * HD:(r + 1) * HD] for i in range(NBL) for r in range(GROUP)],
        axis=0,
    )


def fold(x, op):
    return op(x.reshape(-1, 8, x.shape[-1]), axis=0)


def limits(counts, p):
    row_id = lax.broadcasted_iota(jnp.int32, (2 * BLK, 1), 0)
    return [jnp.where(row_id + 2 * BLK * p < BLK * n, 0.0, NEG) for n in counts]


def masked(raw, bias):
    return jnp.concatenate([raw[:, i * QN:(i + 1) * QN] + bias[i] for i in range(NBL)], axis=1)


def own_kernel(
    info_ref, q_ref, g_ref, own_ref, within_ref,
    q_out, g_out, qt_out, gt_out, e_ref, max_ref, sum_ref,
):
    q = gather(q_ref)
    g = gather(g_ref)
    qt = q.T
    q_out[...] = q
    g_out[...] = g
    qt_out[...] = qt
    gt_out[...] = g.T
    mx = jnp.full((8, WIDE), NEG, jnp.float32)
    for p in range(OWNP):
        k = own_ref[2 * p:2 * p + 2, :, 0].reshape(2 * BLK, HD)
        raw = dot(k, qt, ((1,), (0,))) * (SCALE * LOG2E)
        parts = []
        for half in range(2):
            j = 2 * p + half
            pieces = []
            for i in range(NBL):
                piece = raw[half * BLK:(half + 1) * BLK, i * QN:(i + 1) * QN]
                if j < i:
                    piece = piece + jnp.where(info_ref[2 + i, 1 + j] > 0, 0.0, NEG)
                elif j == i:
                    bias = jnp.where(within_ref[i] > 0.5, 0.0, NEG)
                    piece = piece + jnp.concatenate([bias] * GROUP, axis=1)
                else:
                    piece = jnp.full_like(piece, NEG)
                pieces.append(piece)
            parts.append(jnp.concatenate(pieces, axis=1))
        s = jnp.concatenate(parts, axis=0)
        e_ref[p] = s
        mx = jnp.maximum(mx, fold(s, jnp.max))
    m = jnp.max(mx, axis=0, keepdims=True)
    total = jnp.zeros((8, WIDE), jnp.float32)
    for p in range(OWNP):
        e = jnp.exp2(e_ref[p] - m)
        e_ref[p] = e
        total = total + fold(e, jnp.sum)
    max_ref[...] = m
    sum_ref[...] = jnp.sum(total, axis=0, keepdims=True)


def row_kernel(info_ref, qt_ref, row_ref, e_ref, max_ref, sum_ref, s_s, sems):
    remote = info_ref[0, 0]
    row_first = info_ref[0, 2]
    crossing = info_ref[0, 3]
    pairs = (remote - crossing + 1) // 2
    counts = [info_ref[2 + i, 0] - crossing for i in range(NBL)]

    def scores(p, mx):
        ks = []
        for half in range(2):
            block = info_ref[1, jnp.minimum(crossing + 2 * p + half, MAXD - 1)]
            ks.append(row_ref[jnp.maximum(block - row_first, 0), :, 0].reshape(BLK, HD))
        k = jnp.concatenate(ks, axis=0)
        raw = dot(k, qt_ref[...], ((1,), (0,))) * (SCALE * LOG2E)
        s = masked(raw, limits(counts, p))
        s_s[p] = s
        return jnp.maximum(mx, fold(s, jnp.max))

    mx = lax.fori_loop(0, pairs, scores, jnp.full((8, WIDE), NEG, jnp.float32))
    m = jnp.max(mx, axis=0, keepdims=True)

    def expo(p, total):
        e = jnp.exp2(s_s[p] - m)
        s_s[p] = e
        pltpu.make_async_copy(s_s.at[p], e_ref.at[p], sems.at[p]).start()
        return total + fold(e, jnp.sum)

    total = lax.fori_loop(0, pairs, expo, jnp.zeros((8, WIDE), jnp.float32))
    max_ref[...] = m
    sum_ref[...] = jnp.sum(total, axis=0, keepdims=True)

    def finish(p, carry):
        pltpu.make_async_copy(s_s.at[p], e_ref.at[p], sems.at[p]).wait()
        return carry

    lax.fori_loop(0, pairs, finish, 0)


def kernel(
    info_ref, q_ref, g_ref, qt_ref, gt_ref, own_ref, row_ref,
    mine_ref, next_ref, last_ref, far_ref, near_ref,
    own_max, own_sum, row_max, row_sum, own_e, row_e,
    o_ref, dq_ref, row_grad_ref, mine_grad_ref, next_grad_ref, last_grad_ref, far_grad_ref, near_grad_ref,
    k_s, v_s, kt_s, vt_s, s_s, dk_s, dv_s, acc_s, fac_s, cross_s, cross_grad_s, row_s, zero_s, stage_s, o_s,
    sems, row_sems, zero_sems, stage_sems, o_sem,
):
    remote = info_ref[0, 0]
    row_first = info_ref[0, 2]
    crossing = info_ref[0, 3]
    row_pairs = (remote - crossing + 1) // 2
    cross_pairs = (crossing + 1) // 2
    cross_at = OWNP + row_pairs
    pairs = cross_at + cross_pairs

    def own_copy(p):
        return pltpu.make_async_copy(own_e.at[p], s_s.at[p], sems.at[p])

    def row_copy(p):
        return pltpu.make_async_copy(row_e.at[p], s_s.at[OWNP + p], sems.at[OWNP + p])

    for p in range(OWNP):
        own_copy(p).start()

    def begin(p, carry):
        row_copy(p).start()
        return carry

    def row_place(slot):
        return jnp.maximum(info_ref[1, jnp.minimum(slot, MAXD - 1)] - row_first, 0)

    def fetch(at):
        place = row_place(crossing + at)
        return pltpu.make_async_copy(row_ref.at[place], row_s.at[at], row_sems.at[at])

    def zero(j):
        return pltpu.make_async_copy(
            zero_s, row_grad_ref.at[pl.ds(j * NBL, NBL)], zero_sems.at[j]
        )

    def begin_row(p, carry):
        fetch(2 * p).start()
        fetch(2 * p + 1).start()
        return carry

    lax.fori_loop(0, row_pairs, begin_row, 0)
    lax.fori_loop(0, row_pairs, begin, 0)
    zero_s[...] = jnp.zeros_like(zero_s)
    for j in range(ZN):
        zero(j).start()
    cross_grad_s[...] = jnp.zeros_like(cross_grad_s)
    at = 0
    for ref in (mine_ref, next_ref, last_ref, far_ref, near_ref):
        cross_s[at:at + ref.shape[0]] = ref[...]
        at += ref.shape[0]

    def take(p, half, kv):
        k = kv[:, 0].reshape(BLK, HD)
        v = kv[:, 1].reshape(BLK, HD)
        k_s[p, half * BLK:(half + 1) * BLK, :] = k
        v_s[p, half * BLK:(half + 1) * BLK, :] = v
        kt_s[p, :, half * BLK:(half + 1) * BLK] = k.T
        vt_s[p, :, half * BLK:(half + 1) * BLK] = v.T

    for j in range(NBL):
        take(j // 2, j % 2, own_ref[j])

    def load_row(p, carry):
        for half in range(2):
            fetch(2 * p + half).wait()
            take(OWNP + p, half, row_s[2 * p + half])
        return carry

    lax.fori_loop(0, row_pairs, load_row, 0)

    def load_cross(p, carry):
        for half in range(2):
            take(cross_at + p, half, cross_s[info_ref[6, 2 * p + half]])
        return carry

    lax.fori_loop(0, cross_pairs, load_cross, 0)

    counts = [jnp.minimum(info_ref[2 + i, 0], crossing) for i in range(NBL)]

    def scores(p, mx):
        raw = dot(k_s[cross_at + p], qt_ref[...], ((1,), (0,))) * (SCALE * LOG2E)
        s = masked(raw, limits(counts, p))
        s_s[cross_at + p] = s
        return jnp.maximum(mx, fold(s, jnp.max))

    mx = lax.fori_loop(0, cross_pairs, scores, jnp.full((8, WIDE), NEG, jnp.float32))
    m = jnp.max(mx, axis=0, keepdims=True)
    m = jnp.maximum(m, jnp.maximum(own_max[...], row_max[...]))

    def expo(p, total):
        e = jnp.exp2(s_s[cross_at + p] - m)
        s_s[cross_at + p] = e
        return total + fold(e, jnp.sum)

    total = lax.fori_loop(0, cross_pairs, expo, jnp.zeros((8, WIDE), jnp.float32))
    own_f = jnp.exp2(own_max[...] - m)
    row_f = jnp.exp2(row_max[...] - m)
    total = jnp.sum(total, axis=0, keepdims=True) + own_sum[...] * own_f + row_sum[...] * row_f
    inv = 1.0 / total
    fac_s[0] = own_f * inv
    fac_s[1] = row_f * inv
    fac_s[2] = inv

    acc_s[...] = jnp.zeros_like(acc_s)

    def kind_of(p):
        return jnp.where(p < OWNP, 0, jnp.where(p < cross_at, 1, 2))

    def waited(p):
        @pl.when(p < cross_at)
        def _():
            pltpu.make_async_copy(own_e.at[0], s_s.at[p], sems.at[p]).wait()

    def attend(ps):
        for p in ps:
            waited(p)
        ws = []
        for p in ps:
            w = (s_s[p] * fac_s[kind_of(p)]).astype(jnp.bfloat16)
            dv_s[p] = dot(w, g_ref[...], ((1,), (0,)))
            ws.append(w)
        if len(ps) == 1:
            acc_s[...] += dot(vt_s[ps[0]], ws[0], ((1,), (0,)))
        else:
            vt = jnp.concatenate([vt_s[p] for p in ps], axis=1)
            acc_s[...] += dot(vt, jnp.concatenate(ws, axis=0), ((1,), (0,)))

    def by_two(step):
        def two(t, carry):
            step([2 * t, 2 * t + 1])
            return carry

        lax.fori_loop(0, pairs // 2, two, 0)

        @pl.when(pairs % 2 == 1)
        def _():
            step([pairs - 1])

    by_two(attend)
    ot = acc_s[...].astype(jnp.bfloat16)
    delta = jnp.sum(
        gt_ref[...].astype(jnp.float32) * ot.astype(jnp.float32), axis=0, keepdims=True
    )

    def spread(ref, x):
        for i in range(NBL):
            for r in range(GROUP):
                at = (i * GROUP + r) * BLK
                ref[i * BLK:(i + 1) * BLK, r * HD:(r + 1) * HD] = x[:, at:at + BLK].T

    spread(o_s, ot)
    o_copy = pltpu.make_async_copy(o_s, o_ref, o_sem)
    o_copy.start()
    acc_s[...] = jnp.zeros_like(acc_s)

    def back(ps):
        dss = []
        for p in ps:
            dprob = dot(v_s[p], gt_ref[...], ((1,), (0,)))
            ds = (s_s[p] * fac_s[kind_of(p)] * (dprob - delta)).astype(jnp.bfloat16)
            dk_s[p] = dot(ds, q_ref[...], ((1,), (0,)))
            dss.append(ds)
        if len(ps) == 1:
            acc_s[...] += dot(kt_s[ps[0]], dss[0], ((1,), (0,)))
        else:
            kt = jnp.concatenate([kt_s[p] for p in ps], axis=1)
            acc_s[...] += dot(kt, jnp.concatenate(dss, axis=0), ((1,), (0,)))

    by_two(back)
    spread(dq_ref, (acc_s[...] * SCALE).astype(jnp.bfloat16))

    def put(out_ref, place, p, half):
        rows = pl.ds(half * BLK, BLK)
        dk = dk_s[p, rows, :] * SCALE
        dv = dv_s[p, rows, :]
        out_ref[place, :, 0] = dk.astype(jnp.bfloat16).reshape(2, BLK // 2, HD)
        out_ref[place, :, 1] = dv.astype(jnp.bfloat16).reshape(2, BLK // 2, HD)

    own_place = info_ref[0, 1] - row_first
    own_out = pltpu.make_async_copy(
        stage_s.at[pl.ds(MAXD, NBL)], row_grad_ref.at[pl.ds(own_place, NBL)], stage_sems.at[MAXD]
    )
    for j in range(NBL):
        put(stage_s, MAXD + j, j // 2, j % 2)
    for j in range(ZN):
        zero(j).wait()
    own_out.start()

    def send(at):
        place = row_place(crossing + at)
        return pltpu.make_async_copy(stage_s.at[at], row_grad_ref.at[place], stage_sems.at[at])

    def put_row(at, carry):
        put(stage_s, at, OWNP + at // 2, at % 2)
        send(at).start()
        return carry

    lax.fori_loop(0, remote - crossing, put_row, 0)

    def put_cross(p, carry):
        for half in range(2):
            slot = 2 * p + half

            @pl.when(slot < crossing)
            def _():
                put(cross_grad_s, info_ref[6, slot], cross_at + p, half)

        return carry

    lax.fori_loop(0, cross_pairs, put_cross, 0)
    at = 0
    for ref in (mine_grad_ref, next_grad_ref, last_grad_ref, far_grad_ref, near_grad_ref):
        ref[...] = cross_grad_s[at:at + ref.shape[0]]
        at += ref.shape[0]

    def sent(at, carry):
        send(at).wait()
        return carry

    lax.fori_loop(0, remote - crossing, sent, 0)
    own_out.wait()
    o_copy.wait()


VM = pl.BlockSpec(memory_space=pltpu.VMEM)
SM = pl.BlockSpec(memory_space=pltpu.SMEM)
ANY = pl.BlockSpec(memory_space=pltpu.HBM)
LIMIT = pltpu.CompilerParams(vmem_limit_bytes=58 << 20)


def like(shape, dtype=jnp.bfloat16):
    return jax.ShapeDtypeStruct(shape, dtype)


def own_part(info, q, g, own, within):
    line = like((1, WIDE), jnp.float32)
    return pl.pallas_call(
        own_kernel,
        out_shape=(
            like((WIDE, HD)), like((WIDE, HD)), like((HD, WIDE)), like((HD, WIDE)),
            like((OWNP, 2 * BLK, WIDE), jnp.float32), line, line,
        ),
        in_specs=[SM] + [VM] * 4,
        out_specs=(VM,) * 7,
        compiler_params=LIMIT,
    )(info, q, g, own, within)


def row_part(info, qt, row):
    line = like((1, WIDE), jnp.float32)
    tiles = (MAXD // 2, 2 * BLK, WIDE)
    return pl.pallas_call(
        row_kernel,
        out_shape=(like(tiles, jnp.float32), line, line),
        in_specs=[SM, VM, VM],
        out_specs=(ANY, VM, VM),
        scratch_shapes=[pltpu.VMEM(tiles, jnp.float32), pltpu.SemaphoreType.DMA((MAXD // 2,))],
        compiler_params=LIMIT,
    )(info, qt, row)


def last_part(info, q, own, row, cross, own_stuff, row_stuff):
    qs, gs, qt, gt, own_e, own_max, own_sum = own_stuff
    row_e, row_max, row_sum = row_stuff
    outs = tuple(like(a.shape) for a in (q, q, row, *cross))
    return pl.pallas_call(
        kernel,
        out_shape=outs,
        in_specs=[SM] + [VM] * 5 + [ANY] + [VM] * (4 + len(cross)) + [ANY] * 2,
        out_specs=(ANY, VM, ANY) + (VM,) * len(cross),
        scratch_shapes=[
            pltpu.VMEM((NPAIR, 2 * BLK, HD), jnp.bfloat16),
            pltpu.VMEM((NPAIR, 2 * BLK, HD), jnp.bfloat16),
            pltpu.VMEM((NPAIR, HD, 2 * BLK), jnp.bfloat16),
            pltpu.VMEM((NPAIR, HD, 2 * BLK), jnp.bfloat16),
            pltpu.VMEM((NPAIR, 2 * BLK, WIDE), jnp.float32),
            pltpu.VMEM((NPAIR, 2 * BLK, HD), jnp.float32),
            pltpu.VMEM((NPAIR, 2 * BLK, HD), jnp.float32),
            pltpu.VMEM((HD, WIDE), jnp.float32),
            pltpu.VMEM((3, 1, WIDE), jnp.float32),
            pltpu.VMEM((MAXD,) + own.shape[1:], jnp.bfloat16),
            pltpu.VMEM((MAXD,) + own.shape[1:], jnp.bfloat16),
            pltpu.VMEM((MAXD,) + own.shape[1:], jnp.bfloat16),
            pltpu.VMEM(own.shape, jnp.bfloat16),
            pltpu.VMEM((MAXD + NBL,) + own.shape[1:], jnp.bfloat16),
            pltpu.VMEM(q.shape, jnp.bfloat16),
            pltpu.SemaphoreType.DMA((NPAIR,)),
            pltpu.SemaphoreType.DMA((MAXD,)),
            pltpu.SemaphoreType.DMA((ZN,)),
            pltpu.SemaphoreType.DMA((MAXD + 1,)),
            pltpu.SemaphoreType.DMA,
        ],
        compiler_params=LIMIT,
    )(info, qs, gs, qt, gt, own, row, *cross, own_max, own_sum, row_max, row_sum, own_e, row_e)


def pick_kernel(index_ref, from_ref, *outs):
    for k, out in enumerate(outs):
        for s in range(out.shape[0]):
            out[s] = from_ref[index_ref[k * out.shape[0] + s]]


def pick(index, pool, parts):
    size = index.shape[0] // parts
    return pl.pallas_call(
        pick_kernel,
        out_shape=(like((size,) + pool.shape[1:]),) * parts,
        in_specs=[SM, VM],
        out_specs=(VM,) * parts,
        compiler_params=pltpu.CompilerParams(vmem_limit_bytes=24 << 20),
    )(index, pool)


def merge_kernel(place_ref, lead_ref, row_ref, *rest):
    parts, out_ref, kept, in_sems, out_sems = rest[:-4], rest[-4], rest[-3], rest[-2], rest[-1]
    size = parts[0].shape[0]
    count = size * len(parts)

    def each_lead(step):
        for at in range(count):
            pl.when(lead_ref[at] == at)(functools.partial(step, at))

    def load(at):
        return pltpu.make_async_copy(out_ref.at[place_ref[at]], kept.at[at], in_sems.at[at])

    def store(at):
        return pltpu.make_async_copy(kept.at[at], out_ref.at[place_ref[at]], out_sems.at[at])

    each_lead(lambda at: load(at).start())
    each_lead(lambda at: load(at).wait())
    for at in range(count):

        @pl.when(lead_ref[at] >= 0)
        def _():
            lead = lead_ref[at]
            part = parts[at // size][at % size]
            both = kept[lead].astype(jnp.float32) + part.astype(jnp.float32)
            kept[lead] = both.astype(jnp.bfloat16)

    each_lead(lambda at: store(at).start())
    each_lead(lambda at: store(at).wait())


def merge(place, valid, row_grad, parts):
    count = place.shape[0]
    same = (place[:, None] == place[None, :]) & valid[None, :]
    lead = jnp.where(valid, jnp.argmax(same, axis=1).astype(jnp.int32), -1)
    return pl.pallas_call(
        merge_kernel,
        out_shape=jax.ShapeDtypeStruct(row_grad.shape, row_grad.dtype),
        in_specs=[SM, SM, ANY] + [VM] * len(parts),
        out_specs=ANY,
        input_output_aliases={2: 0},
        scratch_shapes=[
            pltpu.VMEM((count,) + row_grad.shape[1:], row_grad.dtype),
            pltpu.SemaphoreType.DMA((count,)),
            pltpu.SemaphoreType.DMA((count,)),
        ],
        compiler_params=pltpu.CompilerParams(vmem_limit_bytes=62 << 20),
    )(place, lead, row_grad, *parts)


ROW = ZN * NBL
SETS = 4
SLOTS = MAXD // SETS
Z_GROUPS = [[y * ZN + z for z in range(ZN)] for y in range(YN)]


def along(x, k):
    pairs = [(y * ZN + z, y * ZN + (z + k) % ZN) for y in range(YN) for z in range(ZN)]
    return lax.ppermute(x, "ctx", pairs)


def up(x, k):
    pairs = [(y * ZN + z, (y + k) * ZN + z) for y in range(YN - k) for z in range(ZN)]
    return lax.ppermute(x, "ctx", pairs)


def down(x, k):
    pairs = [((y + k) * ZN + z, y * ZN + z) for y in range(YN - k) for z in range(ZN)]
    return lax.ppermute(x, "ctx", pairs)


def info_of(ancestors, c, y, z):
    first = c * NBL
    row_first = y * ROW
    lists = lax.dynamic_slice_in_dim(ancestors, first, NBL, 0)
    remote = jnp.sum(((lists >= 0) & (lists < first)).astype(jnp.int32), axis=1)
    crossing = jnp.sum(((lists[0] >= 0) & (lists[0] < row_first)).astype(jnp.int32))
    own = first + jnp.arange(NBL, dtype=jnp.int32)
    flags = jnp.any(lists[:, None, :] == own[None, :, None], axis=2).astype(jnp.int32)
    head = jnp.concatenate(
        [jnp.stack([remote[0], first, row_first, crossing]), jnp.zeros((MAXD - 4,), jnp.int32)]
    )[None]
    rest = jnp.concatenate([remote[:, None], flags, jnp.zeros((NBL, MAXD - 1 - NBL), jnp.int32)], axis=1)
    slot = jnp.arange(MAXD, dtype=jnp.int32)
    turn = (slot // SLOTS - z) % SETS
    base = jnp.array([0, SLOTS, 3 * SLOTS, 2 * SLOTS], jnp.int32)
    place = (base[turn] + slot % SLOTS)[None]
    return jnp.concatenate([head, lists[:1], rest, place], axis=0)


def body(queries, keys, values, out_grad, ancestors, parents):
    tokens = queries.shape[0]
    groups = keys.shape[1]
    c = lax.axis_index("ctx")
    y = c // ZN
    z = c % ZN
    row_lists = ancestors[::ROW]
    slots = lax.dynamic_slice_in_dim(row_lists, (z % SETS) * SLOTS, SLOTS, 1)
    slot_rows = jnp.where(slots >= 0, slots // ROW, -1)
    my_rows = lax.dynamic_index_in_dim(slot_rows, y, 0, keepdims=False)

    kv = jnp.stack([keys, values]).transpose(2, 0, 1, 3)
    kv = lax.all_to_all(kv, "head", split_axis=0, concat_axis=0, tiled=True)
    own = kv.reshape(NBL, 2, 2, BLK // 2, HD)
    row = lax.all_gather(own, "ctx", axis=0, axis_index_groups=Z_GROUPS, tiled=True)
    q = lax.all_to_all(queries.reshape(tokens, -1), "head", split_axis=1, concat_axis=0, tiled=True)
    g = lax.all_to_all(out_grad.reshape(tokens, -1), "head", split_axis=1, concat_axis=0, tiled=True)

    row, q, g = lax.optimization_barrier((row, q, g))

    def of_row(k):
        return lax.dynamic_index_in_dim(slots, jnp.minimum(y + k, YN - 1), 0, keepdims=False)

    within = tree_reach_t(parents)
    info = info_of(ancestors, c, y, z)
    wanted = [jnp.clip(of_row(k) - y * ROW, 0, ROW - 1) for k in range(1, YN)]
    sent = pick(jnp.concatenate(wanted), row, YN - 1)
    sent, q, g = lax.optimization_barrier((sent, q, g))
    moved = [up(sent[k - 1], k) for k in range(1, YN)]
    own_stuff = own_part(info, q, g, own, within)
    moved, own_stuff = lax.optimization_barrier((moved, own_stuff))
    mine = jnp.zeros((SLOTS,) + own.shape[1:], own.dtype)
    for k in range(1, YN):
        here = (my_rows == y - k)[:, None, None, None, None]
        mine = jnp.where(here, moved[k - 1], mine)
    half = SLOTS // 2
    cross = (mine, along(mine, -1), along(mine, 1), along(mine[:half], -2), along(mine[half:], 2))
    row_stuff = row_part(info, own_stuff[2], row)
    o, dq, row_grad, *turns = last_part(info, q, own, row, cross, own_stuff, row_stuff)

    here = turns[0].astype(jnp.float32)
    here = here + along(turns[1], 1).astype(jnp.float32) + along(turns[2], -1).astype(jnp.float32)
    far = jnp.concatenate([along(turns[3], 2), along(turns[4], -2)], axis=0)
    here = (here + far.astype(jnp.float32)).astype(jnp.bfloat16)
    places, valids, parts = [], [], []
    for k in range(1, YN):
        parts.append(down(here, k))
        theirs = of_row(k)
        valid = (theirs >= 0) & (theirs // ROW == y) & (y + k < YN)
        places.append(jnp.where(valid, theirs - y * ROW, 0))
        valids.append(valid)
    row_grad = merge(jnp.concatenate(places), jnp.concatenate(valids), row_grad, parts)
    row_grad, o, dq = lax.optimization_barrier((row_grad, o, dq))
    grad = lax.psum_scatter(
        row_grad, "ctx", scatter_dimension=0, axis_index_groups=Z_GROUPS, tiled=True
    )
    o = lax.all_to_all(o, "head", split_axis=0, concat_axis=1, tiled=True)
    dq = lax.all_to_all(dq, "head", split_axis=0, concat_axis=1, tiled=True)
    grad, o, dq = lax.optimization_barrier((grad, o, dq))
    grad = grad.reshape(groups, 2, BLK // 2, HD)
    grad = lax.all_to_all(grad, "head", split_axis=0, concat_axis=0, tiled=True)
    grad = grad.transpose(1, 2, 0, 3)
    shape = queries.shape
    return (o.reshape(shape), dq.reshape(shape), grad[0], grad[1])


def solution(mesh):
    rows = P(("ctx", "head"), None, None)
    return jax.shard_map(
        body,
        mesh=mesh,
        in_specs=(rows, rows, rows, rows, P(), P("ctx", None)),
        out_specs=(rows, rows, rows, rows),
        check_vma=False,
    )
```

```python
import functools
import math

import jax
import jax.numpy as jnp
from jax import lax
from jax.experimental import pallas as pl
from jax.experimental.pallas import tpu as pltpu
from jax.sharding import PartitionSpec as P

HD = 128
GROUP = 5
BLK = 128
NBL = 4
MAXD = 16
QN = GROUP * BLK
SCALE = 1.0 / math.sqrt(HD)
LOG2E = 1.0 / math.log(2.0)
NEG = -1e30
OWNP = NBL // 2
NPAIR = OWNP + MAXD // 2 + 1
WIDE = NBL * QN
YN = 4
ZN = 8


def tree_reach_t(parents):
    block_width = parents.shape[-1]
    hops = parents[:, None, :] == jnp.arange(block_width, dtype=jnp.int32)[None, :, None]
    eye = jnp.eye(block_width, dtype=jnp.bool_)[None]
    reached = (hops | eye).astype(jnp.bfloat16)
    for _ in range(max(1, (block_width - 1).bit_length())):
        product = jnp.einsum("bts,bsu->btu", reached, reached, preferred_element_type=jnp.float32)
        reached = jnp.minimum(product, 1.0).astype(jnp.bfloat16)
    return reached.astype(jnp.float32)


def dot(a, b, dims):
    return lax.dot_general(a, b, (dims, ((), ())), preferred_element_type=jnp.float32)


def gather(ref):
    return jnp.concatenate(
        [ref[i * BLK:(i + 1) * BLK, r * HD:(r + 1) * HD] for i in range(NBL) for r in range(GROUP)],
        axis=0,
    )


def fold(x, op):
    return op(x.reshape(-1, 8, x.shape[-1]), axis=0)


def limits(counts, p):
    row_id = lax.broadcasted_iota(jnp.int32, (2 * BLK, 1), 0)
    return [jnp.where(row_id + 2 * BLK * p < BLK * n, 0.0, NEG) for n in counts]


def masked(raw, bias):
    return jnp.concatenate([raw[:, i * QN:(i + 1) * QN] + bias[i] for i in range(NBL)], axis=1)


def own_kernel(
    info_ref, q_ref, g_ref, own_ref, within_ref,
    q_out, g_out, qt_out, gt_out, e_ref, max_ref, sum_ref,
):
    q = gather(q_ref)
    g = gather(g_ref)
    qt = q.T
    q_out[...] = q
    g_out[...] = g
    qt_out[...] = qt
    gt_out[...] = g.T
    mx = jnp.full((8, WIDE), NEG, jnp.float32)
    for p in range(OWNP):
        k = own_ref[2 * p:2 * p + 2, :, 0].reshape(2 * BLK, HD)
        raw = dot(k, qt, ((1,), (0,))) * (SCALE * LOG2E)
        parts = []
        for half in range(2):
            j = 2 * p + half
            pieces = []
            for i in range(NBL):
                piece = raw[half * BLK:(half + 1) * BLK, i * QN:(i + 1) * QN]
                if j < i:
                    piece = piece + jnp.where(info_ref[2 + i, 1 + j] > 0, 0.0, NEG)
                elif j == i:
                    bias = jnp.where(within_ref[i] > 0.5, 0.0, NEG)
                    piece = piece + jnp.concatenate([bias] * GROUP, axis=1)
                else:
                    piece = jnp.full_like(piece, NEG)
                pieces.append(piece)
            parts.append(jnp.concatenate(pieces, axis=1))
        s = jnp.concatenate(parts, axis=0)
        e_ref[p] = s
        mx = jnp.maximum(mx, fold(s, jnp.max))
    m = jnp.max(mx, axis=0, keepdims=True)
    total = jnp.zeros((8, WIDE), jnp.float32)
    for p in range(OWNP):
        e = jnp.exp2(e_ref[p] - m)
        e_ref[p] = e
        total = total + fold(e, jnp.sum)
    max_ref[...] = m
    sum_ref[...] = jnp.sum(total, axis=0, keepdims=True)


def row_kernel(info_ref, qt_ref, row_ref, e_ref, max_ref, sum_ref, s_s, sems):
    remote = info_ref[0, 0]
    row_first = info_ref[0, 2]
    crossing = info_ref[0, 3]
    pairs = (remote - crossing + 1) // 2
    counts = [info_ref[2 + i, 0] - crossing for i in range(NBL)]

    def scores(p, mx):
        ks = []
        for half in range(2):
            block = info_ref[1, jnp.minimum(crossing + 2 * p + half, MAXD - 1)]
            ks.append(row_ref[jnp.maximum(block - row_first, 0), :, 0].reshape(BLK, HD))
        k = jnp.concatenate(ks, axis=0)
        raw = dot(k, qt_ref[...], ((1,), (0,))) * (SCALE * LOG2E)
        s = masked(raw, limits(counts, p))
        s_s[p] = s
        return jnp.maximum(mx, fold(s, jnp.max))

    mx = lax.fori_loop(0, pairs, scores, jnp.full((8, WIDE), NEG, jnp.float32))
    m = jnp.max(mx, axis=0, keepdims=True)

    def expo(p, total):
        e = jnp.exp2(s_s[p] - m)
        s_s[p] = e
        pltpu.make_async_copy(s_s.at[p], e_ref.at[p], sems.at[p]).start()
        return total + fold(e, jnp.sum)

    total = lax.fori_loop(0, pairs, expo, jnp.zeros((8, WIDE), jnp.float32))
    max_ref[...] = m
    sum_ref[...] = jnp.sum(total, axis=0, keepdims=True)

    def finish(p, carry):
        pltpu.make_async_copy(s_s.at[p], e_ref.at[p], sems.at[p]).wait()
        return carry

    lax.fori_loop(0, pairs, finish, 0)


def kernel(
    info_ref, q_ref, g_ref, qt_ref, gt_ref, own_ref, row_ref,
    mine_ref, next_ref, last_ref, far_ref, near_ref,
    own_max, own_sum, row_max, row_sum, own_e, row_e,
    o_ref, dq_ref, row_grad_ref, mine_grad_ref, next_grad_ref, last_grad_ref, far_grad_ref, near_grad_ref,
    k_s, v_s, kt_s, vt_s, s_s, dk_s, dv_s, acc_s, fac_s, cross_s, cross_grad_s, row_s, zero_s, stage_s, o_s,
    sems, row_sems, zero_sems, stage_sems, o_sem,
):
    remote = info_ref[0, 0]
    row_first = info_ref[0, 2]
    crossing = info_ref[0, 3]
    row_pairs = (remote - crossing + 1) // 2
    cross_pairs = (crossing + 1) // 2
    cross_at = OWNP + row_pairs
    pairs = cross_at + cross_pairs

    def own_copy(p):
        return pltpu.make_async_copy(own_e.at[p], s_s.at[p], sems.at[p])

    def row_copy(p):
        return pltpu.make_async_copy(row_e.at[p], s_s.at[OWNP + p], sems.at[OWNP + p])

    for p in range(OWNP):
        own_copy(p).start()

    def begin(p, carry):
        row_copy(p).start()
        return carry

    def row_place(slot):
        return jnp.maximum(info_ref[1, jnp.minimum(slot, MAXD - 1)] - row_first, 0)

    def fetch(at):
        place = row_place(crossing + at)
        return pltpu.make_async_copy(row_ref.at[place], row_s.at[at], row_sems.at[at])

    def zero(j):
        return pltpu.make_async_copy(
            zero_s, row_grad_ref.at[pl.ds(j * NBL, NBL)], zero_sems.at[j]
        )

    def begin_row(p, carry):
        fetch(2 * p).start()
        fetch(2 * p + 1).start()
        return carry

    lax.fori_loop(0, row_pairs, begin_row, 0)
    lax.fori_loop(0, row_pairs, begin, 0)
    zero_s[...] = jnp.zeros_like(zero_s)
    for j in range(ZN):
        zero(j).start()
    cross_grad_s[...] = jnp.zeros_like(cross_grad_s)
    at = 0
    for ref in (mine_ref, next_ref, last_ref, far_ref, near_ref):
        cross_s[at:at + ref.shape[0]] = ref[...]
        at += ref.shape[0]

    def take(p, first, second):
        k = jnp.concatenate([kv[:, 0].reshape(BLK, HD) for kv in (first, second)], axis=0)
        v = jnp.concatenate([kv[:, 1].reshape(BLK, HD) for kv in (first, second)], axis=0)
        k_s[p] = k
        v_s[p] = v
        kt_s[p] = k.T
        vt_s[p] = v.T
        return k

    for p in range(OWNP):
        take(p, own_ref[2 * p], own_ref[2 * p + 1])

    def load_row(p, carry):
        fetch(2 * p).wait()
        fetch(2 * p + 1).wait()
        take(OWNP + p, row_s[2 * p], row_s[2 * p + 1])
        return carry

    lax.fori_loop(0, row_pairs, load_row, 0)

    counts = [jnp.minimum(info_ref[2 + i, 0], crossing) for i in range(NBL)]

    def scores(p, mx):
        places = [info_ref[6, 2 * p + half] for half in range(2)]
        k = take(cross_at + p, cross_s[places[0]], cross_s[places[1]])
        raw = dot(k, qt_ref[...], ((1,), (0,))) * (SCALE * LOG2E)
        s = masked(raw, limits(counts, p))
        s_s[cross_at + p] = s
        return jnp.maximum(mx, fold(s, jnp.max))

    mx = lax.fori_loop(0, cross_pairs, scores, jnp.full((8, WIDE), NEG, jnp.float32))
    m = jnp.max(mx, axis=0, keepdims=True)
    m = jnp.maximum(m, jnp.maximum(own_max[...], row_max[...]))

    def expo(p, total):
        e = jnp.exp2(s_s[cross_at + p] - m)
        s_s[cross_at + p] = e
        return total + fold(e, jnp.sum)

    total = lax.fori_loop(0, cross_pairs, expo, jnp.zeros((8, WIDE), jnp.float32))
    own_f = jnp.exp2(own_max[...] - m)
    row_f = jnp.exp2(row_max[...] - m)
    total = jnp.sum(total, axis=0, keepdims=True) + own_sum[...] * own_f + row_sum[...] * row_f
    inv = 1.0 / total
    fac_s[0] = own_f * inv
    fac_s[1] = row_f * inv
    fac_s[2] = inv


    def kind_of(p):
        return jnp.where(p < OWNP, 0, jnp.where(p < cross_at, 1, 2))

    def waited(p):
        @pl.when(p < cross_at)
        def _():
            pltpu.make_async_copy(own_e.at[0], s_s.at[p], sems.at[p]).wait()

    def attend(ps):
        for p in ps:
            waited(p)
        ws = []
        for p in ps:
            w = (s_s[p] * fac_s[kind_of(p)]).astype(jnp.bfloat16)
            dv_s[p] = dot(w, g_ref[...], ((1,), (0,))).astype(jnp.bfloat16)
            ws.append(w)
        if len(ps) == 1:
            acc_s[...] += dot(vt_s[ps[0]], ws[0], ((1,), (0,)))
        else:
            vt = jnp.concatenate([vt_s[p] for p in ps], axis=1)
            acc_s[...] += dot(vt, jnp.concatenate(ws, axis=0), ((1,), (0,)))

    def by_two(step):
        def two(t, carry):
            step([2 * t, 2 * t + 1])
            return carry

        lax.fori_loop(OWNP // 2, pairs // 2, two, 0)

        @pl.when(pairs % 2 == 1)
        def _():
            step([pairs - 1])

    mid = WIDE // 2
    left, right = slice(0, mid), slice(mid, WIDE)

    def halves(out_s, table, first, second, x_ref, finish):
        a, b = first()
        c = second()
        out_s[0] = finish(dot(a, x_ref[left, :], ((1,), (0,))) + dot(b, x_ref[right, :], ((1,), (0,))))
        out_s[1] = finish(dot(c, x_ref[right, :], ((1,), (0,))))
        both = jnp.concatenate([table[0], table[1]], axis=1)
        acc_s[:, left] = dot(table[0], a, ((1,), (0,)))
        acc_s[:, right] = dot(both, jnp.concatenate([b, c], axis=0), ((1,), (0,)))

    def weight(p, cols):
        return (s_s[p, :, cols] * fac_s[0, :, cols]).astype(jnp.bfloat16)

    for p in range(OWNP):
        waited(p)
    halves(
        dv_s, vt_s, lambda: (weight(0, left), weight(0, right)), lambda: weight(1, right),
        g_ref, lambda x: x.astype(jnp.bfloat16),
    )
    by_two(attend)
    ot = acc_s[...].astype(jnp.bfloat16)
    delta = jnp.sum(
        gt_ref[...].astype(jnp.float32) * ot.astype(jnp.float32), axis=0, keepdims=True
    )

    def spread(ref, x):
        for i in range(NBL):
            for r in range(GROUP):
                at = (i * GROUP + r) * BLK
                ref[i * BLK:(i + 1) * BLK, r * HD:(r + 1) * HD] = x[:, at:at + BLK].T

    spread(o_s, ot)
    o_copy = pltpu.make_async_copy(o_s, o_ref, o_sem)
    o_copy.start()

    def back(ps):
        dss = []
        for p in ps:
            dprob = dot(v_s[p], gt_ref[...], ((1,), (0,)))
            ds = (s_s[p] * fac_s[kind_of(p)] * (dprob - delta)).astype(jnp.bfloat16)
            dk_s[p] = (dot(ds, q_ref[...], ((1,), (0,))) * SCALE).astype(jnp.bfloat16)
            dss.append(ds)
        if len(ps) == 1:
            acc_s[...] += dot(kt_s[ps[0]], dss[0], ((1,), (0,)))
        else:
            kt = jnp.concatenate([kt_s[p] for p in ps], axis=1)
            acc_s[...] += dot(kt, jnp.concatenate(dss, axis=0), ((1,), (0,)))

    def slope(p, cols):
        dprob = dot(v_s[p], gt_ref[:, cols], ((1,), (0,)))
        prob = s_s[p, :, cols] * fac_s[0, :, cols]
        return (prob * (dprob - delta[:, cols])).astype(jnp.bfloat16)

    halves(
        dk_s, kt_s, lambda: (slope(0, left), slope(0, right)), lambda: slope(1, right),
        q_ref, lambda x: (x * SCALE).astype(jnp.bfloat16),
    )
    by_two(back)
    spread(dq_ref, (acc_s[...] * SCALE).astype(jnp.bfloat16))

    def put(out_ref, place, p, half):
        rows = pl.ds(half * BLK, BLK)
        dk = dk_s[p, rows, :]
        dv = dv_s[p, rows, :]
        out_ref[place, :, 0] = dk.reshape(2, BLK // 2, HD)
        out_ref[place, :, 1] = dv.reshape(2, BLK // 2, HD)

    own_place = info_ref[0, 1] - row_first
    own_out = pltpu.make_async_copy(
        stage_s.at[pl.ds(MAXD, NBL)], row_grad_ref.at[pl.ds(own_place, NBL)], stage_sems.at[MAXD]
    )
    for j in range(NBL):
        put(stage_s, MAXD + j, j // 2, j % 2)
    for j in range(ZN):
        zero(j).wait()
    own_out.start()

    def send(at):
        place = row_place(crossing + at)
        return pltpu.make_async_copy(stage_s.at[at], row_grad_ref.at[place], stage_sems.at[at])

    def put_row(at, carry):
        put(stage_s, at, OWNP + at // 2, at % 2)
        send(at).start()
        return carry

    lax.fori_loop(0, remote - crossing, put_row, 0)

    def put_cross(p, carry):
        for half in range(2):
            slot = 2 * p + half

            @pl.when(slot < crossing)
            def _():
                put(cross_grad_s, info_ref[6, slot], cross_at + p, half)

        return carry

    lax.fori_loop(0, cross_pairs, put_cross, 0)
    at = 0
    for ref in (mine_grad_ref, next_grad_ref, last_grad_ref, far_grad_ref, near_grad_ref):
        ref[...] = cross_grad_s[at:at + ref.shape[0]]
        at += ref.shape[0]

    def sent(at, carry):
        send(at).wait()
        return carry

    lax.fori_loop(0, remote - crossing, sent, 0)
    own_out.wait()
    o_copy.wait()


VM = pl.BlockSpec(memory_space=pltpu.VMEM)
SM = pl.BlockSpec(memory_space=pltpu.SMEM)
ANY = pl.BlockSpec(memory_space=pltpu.HBM)
LIMIT = pltpu.CompilerParams(vmem_limit_bytes=58 << 20)


def like(shape, dtype=jnp.bfloat16):
    return jax.ShapeDtypeStruct(shape, dtype)


def own_part(info, q, g, own, within):
    line = like((1, WIDE), jnp.float32)
    return pl.pallas_call(
        own_kernel,
        out_shape=(
            like((WIDE, HD)), like((WIDE, HD)), like((HD, WIDE)), like((HD, WIDE)),
            like((OWNP, 2 * BLK, WIDE), jnp.float32), line, line,
        ),
        in_specs=[SM] + [VM] * 4,
        out_specs=(VM,) * 7,
        compiler_params=LIMIT,
    )(info, q, g, own, within)


def row_part(info, qt, row):
    line = like((1, WIDE), jnp.float32)
    tiles = (MAXD // 2, 2 * BLK, WIDE)
    return pl.pallas_call(
        row_kernel,
        out_shape=(like(tiles, jnp.float32), line, line),
        in_specs=[SM, VM, VM],
        out_specs=(ANY, VM, VM),
        scratch_shapes=[pltpu.VMEM(tiles, jnp.float32), pltpu.SemaphoreType.DMA((MAXD // 2,))],
        compiler_params=LIMIT,
    )(info, qt, row)


def last_part(info, q, own, row, cross, own_stuff, row_stuff):
    qs, gs, qt, gt, own_e, own_max, own_sum = own_stuff
    row_e, row_max, row_sum = row_stuff
    outs = tuple(like(a.shape) for a in (q, q, row, *cross))
    return pl.pallas_call(
        kernel,
        out_shape=outs,
        in_specs=[SM] + [VM] * 5 + [ANY] + [VM] * (4 + len(cross)) + [ANY] * 2,
        out_specs=(ANY, VM, ANY) + (VM,) * len(cross),
        scratch_shapes=[
            pltpu.VMEM((NPAIR, 2 * BLK, HD), jnp.bfloat16),
            pltpu.VMEM((NPAIR, 2 * BLK, HD), jnp.bfloat16),
            pltpu.VMEM((NPAIR, HD, 2 * BLK), jnp.bfloat16),
            pltpu.VMEM((NPAIR, HD, 2 * BLK), jnp.bfloat16),
            pltpu.VMEM((NPAIR, 2 * BLK, WIDE), jnp.float32),
            pltpu.VMEM((NPAIR, 2 * BLK, HD), jnp.bfloat16),
            pltpu.VMEM((NPAIR, 2 * BLK, HD), jnp.bfloat16),
            pltpu.VMEM((HD, WIDE), jnp.float32),
            pltpu.VMEM((3, 1, WIDE), jnp.float32),
            pltpu.VMEM((MAXD,) + own.shape[1:], jnp.bfloat16),
            pltpu.VMEM((MAXD,) + own.shape[1:], jnp.bfloat16),
            pltpu.VMEM((MAXD,) + own.shape[1:], jnp.bfloat16),
            pltpu.VMEM(own.shape, jnp.bfloat16),
            pltpu.VMEM((MAXD + NBL,) + own.shape[1:], jnp.bfloat16),
            pltpu.VMEM(q.shape, jnp.bfloat16),
            pltpu.SemaphoreType.DMA((NPAIR,)),
            pltpu.SemaphoreType.DMA((MAXD,)),
            pltpu.SemaphoreType.DMA((ZN,)),
            pltpu.SemaphoreType.DMA((MAXD + 1,)),
            pltpu.SemaphoreType.DMA,
        ],
        compiler_params=LIMIT,
    )(info, qs, gs, qt, gt, own, row, *cross, own_max, own_sum, row_max, row_sum, own_e, row_e)


def pick_kernel(index_ref, from_ref, *outs):
    for k, out in enumerate(outs):
        for s in range(out.shape[0]):
            out[s] = from_ref[index_ref[k * out.shape[0] + s]]


def pick(index, pool, parts):
    size = index.shape[0] // parts
    return pl.pallas_call(
        pick_kernel,
        out_shape=(like((size,) + pool.shape[1:]),) * parts,
        in_specs=[SM, VM],
        out_specs=(VM,) * parts,
        compiler_params=pltpu.CompilerParams(vmem_limit_bytes=24 << 20),
    )(index, pool)


def merge_kernel(place_ref, lead_ref, row_ref, *rest):
    parts, out_ref, kept, in_sems, out_sems = rest[:-4], rest[-4], rest[-3], rest[-2], rest[-1]
    size = parts[0].shape[0]
    count = size * len(parts)

    def each_lead(step):
        for at in range(count):
            pl.when(lead_ref[at] == at)(functools.partial(step, at))

    def load(at):
        return pltpu.make_async_copy(out_ref.at[place_ref[at]], kept.at[at], in_sems.at[at])

    def store(at):
        return pltpu.make_async_copy(kept.at[at], out_ref.at[place_ref[at]], out_sems.at[at])

    each_lead(lambda at: load(at).start())
    each_lead(lambda at: load(at).wait())
    for at in range(count):

        @pl.when(lead_ref[at] >= 0)
        def _():
            lead = lead_ref[at]
            part = parts[at // size][at % size]
            both = kept[lead].astype(jnp.float32) + part.astype(jnp.float32)
            kept[lead] = both.astype(jnp.bfloat16)

    each_lead(lambda at: store(at).start())
    each_lead(lambda at: store(at).wait())


def merge(place, valid, row_grad, parts):
    count = place.shape[0]
    same = (place[:, None] == place[None, :]) & valid[None, :]
    lead = jnp.where(valid, jnp.argmax(same, axis=1).astype(jnp.int32), -1)
    return pl.pallas_call(
        merge_kernel,
        out_shape=jax.ShapeDtypeStruct(row_grad.shape, row_grad.dtype),
        in_specs=[SM, SM, ANY] + [VM] * len(parts),
        out_specs=ANY,
        input_output_aliases={2: 0},
        scratch_shapes=[
            pltpu.VMEM((count,) + row_grad.shape[1:], row_grad.dtype),
            pltpu.SemaphoreType.DMA((count,)),
            pltpu.SemaphoreType.DMA((count,)),
        ],
        compiler_params=pltpu.CompilerParams(vmem_limit_bytes=62 << 20),
    )(place, lead, row_grad, *parts)


ROW = ZN * NBL
SETS = 4
SLOTS = MAXD // SETS
Z_GROUPS = [[y * ZN + z for z in range(ZN)] for y in range(YN)]


def along(x, k):
    pairs = [(y * ZN + z, y * ZN + (z + k) % ZN) for y in range(YN) for z in range(ZN)]
    return lax.ppermute(x, "ctx", pairs)


def up(x, k):
    pairs = [(y * ZN + z, (y + k) * ZN + z) for y in range(YN - k) for z in range(ZN)]
    return lax.ppermute(x, "ctx", pairs)


def down(x, k):
    pairs = [((y + k) * ZN + z, y * ZN + z) for y in range(YN - k) for z in range(ZN)]
    return lax.ppermute(x, "ctx", pairs)


def info_of(ancestors, c, y, z):
    first = c * NBL
    row_first = y * ROW
    lists = lax.dynamic_slice_in_dim(ancestors, first, NBL, 0)
    remote = jnp.sum(((lists >= 0) & (lists < first)).astype(jnp.int32), axis=1)
    crossing = jnp.sum(((lists[0] >= 0) & (lists[0] < row_first)).astype(jnp.int32))
    own = first + jnp.arange(NBL, dtype=jnp.int32)
    flags = jnp.any(lists[:, None, :] == own[None, :, None], axis=2).astype(jnp.int32)
    head = jnp.concatenate(
        [jnp.stack([remote[0], first, row_first, crossing]), jnp.zeros((MAXD - 4,), jnp.int32)]
    )[None]
    rest = jnp.concatenate([remote[:, None], flags, jnp.zeros((NBL, MAXD - 1 - NBL), jnp.int32)], axis=1)
    slot = jnp.arange(MAXD, dtype=jnp.int32)
    turn = (slot // SLOTS - z) % SETS
    base = jnp.array([0, SLOTS, 3 * SLOTS, 2 * SLOTS], jnp.int32)
    place = (base[turn] + slot % SLOTS)[None]
    return jnp.concatenate([head, lists[:1], rest, place], axis=0)


def body(queries, keys, values, out_grad, ancestors, parents):
    tokens = queries.shape[0]
    groups = keys.shape[1]
    c = lax.axis_index("ctx")
    y = c // ZN
    z = c % ZN
    row_lists = ancestors[::ROW]
    slots = lax.dynamic_slice_in_dim(row_lists, (z % SETS) * SLOTS, SLOTS, 1)
    slot_rows = jnp.where(slots >= 0, slots // ROW, -1)
    my_rows = lax.dynamic_index_in_dim(slot_rows, y, 0, keepdims=False)

    kv = jnp.stack([keys, values]).transpose(2, 0, 1, 3)
    kv = lax.all_to_all(kv, "head", split_axis=0, concat_axis=0, tiled=True)
    own = kv.reshape(NBL, 2, 2, BLK // 2, HD)
    row = lax.all_gather(own, "ctx", axis=0, axis_index_groups=Z_GROUPS, tiled=True)
    q = lax.all_to_all(queries.reshape(tokens, -1), "head", split_axis=1, concat_axis=0, tiled=True)
    g = lax.all_to_all(out_grad.reshape(tokens, -1), "head", split_axis=1, concat_axis=0, tiled=True)

    row, q, g = lax.optimization_barrier((row, q, g))

    def of_row(k):
        return lax.dynamic_index_in_dim(slots, jnp.minimum(y + k, YN - 1), 0, keepdims=False)

    within = tree_reach_t(parents)
    info = info_of(ancestors, c, y, z)
    wanted = [jnp.clip(of_row(k) - y * ROW, 0, ROW - 1) for k in range(1, YN)]
    sent = pick(jnp.concatenate(wanted), row, YN - 1)
    sent, q, g = lax.optimization_barrier((sent, q, g))
    moved = [up(sent[k - 1], k) for k in range(1, YN)]
    own_stuff = own_part(info, q, g, own, within)
    moved, own_stuff = lax.optimization_barrier((moved, own_stuff))
    mine = jnp.zeros((SLOTS,) + own.shape[1:], own.dtype)
    for k in range(1, YN):
        here = (my_rows == y - k)[:, None, None, None, None]
        mine = jnp.where(here, moved[k - 1], mine)
    half = SLOTS // 2
    cross = (mine, along(mine, -1), along(mine, 1), along(mine[:half], -2), along(mine[half:], 2))
    row_stuff = row_part(info, own_stuff[2], row)
    o, dq, row_grad, *turns = last_part(info, q, own, row, cross, own_stuff, row_stuff)

    here = turns[0].astype(jnp.float32)
    here = here + along(turns[1], 1).astype(jnp.float32) + along(turns[2], -1).astype(jnp.float32)
    far = jnp.concatenate([along(turns[3], 2), along(turns[4], -2)], axis=0)
    here = (here + far.astype(jnp.float32)).astype(jnp.bfloat16)
    places, valids, parts = [], [], []
    for k in range(1, YN):
        parts.append(down(here, k))
        theirs = of_row(k)
        valid = (theirs >= 0) & (theirs // ROW == y) & (y + k < YN)
        places.append(jnp.where(valid, theirs - y * ROW, 0))
        valids.append(valid)
    row_grad = merge(jnp.concatenate(places), jnp.concatenate(valids), row_grad, parts)
    row_grad, o, dq = lax.optimization_barrier((row_grad, o, dq))
    grad = lax.psum_scatter(
        row_grad, "ctx", scatter_dimension=0, axis_index_groups=Z_GROUPS, tiled=True
    )
    o = lax.all_to_all(o, "head", split_axis=0, concat_axis=1, tiled=True)
    dq = lax.all_to_all(dq, "head", split_axis=0, concat_axis=1, tiled=True)
    grad, o, dq = lax.optimization_barrier((grad, o, dq))
    grad = grad.reshape(groups, 2, BLK // 2, HD)
    grad = lax.all_to_all(grad, "head", split_axis=0, concat_axis=0, tiled=True)
    grad = grad.transpose(1, 2, 0, 3)
    shape = queries.shape
    return (o.reshape(shape), dq.reshape(shape), grad[0], grad[1])


def solution(mesh):
    rows = P(("ctx", "head"), None, None)
    return jax.shard_map(
        body,
        mesh=mesh,
        in_specs=(rows, rows, rows, rows, P(), P("ctx", None)),
        out_specs=(rows, rows, rows, rows),
        check_vma=False,
    )
```
